512 devices in a mesh: row: 32 (over x_lo, z, core), col: 16 (over x_hi, y).
Axes of the slice: x: 4 (x_hi: 2, x_lo: 2; x = x_hi * 2 + x_lo), y: 8, z: 8, core: 2. Of those that a mesh axis runs over, the one named last changes fastest.
Arguments:
- users: float32 [32768, 256], P(('row', 'col')), may hold values from -6 to 6
- items: float32 [32768, 256], P(('col', 'row')), may hold values from -0.75 to 0.75
- tiles: bfloat16 [32, 16, 4, 256, 256], P('row', 'col'), may hold values from -0.03125 to 0.03125
- tile_pos: int32 [32, 16, 4], P('row', 'col'), may hold values from 0 to 31, as said below
- tile_count: int32 [32, 16], P('row', 'col'), may hold values from 1 to 4, as said below
- user_ids: int32 [131072], P(('row', 'col')), may hold values from 0 to 32767, as said below
- pos_ids: int32 [131072], P(('row', 'col')), may hold values from 0 to 32767, as said below
- neg_ids: int32 [131072], P(('row', 'col')), may hold values from 0 to 32767, as said below
Outputs:
- grad_users: float32 [32768, 256], P(('row', 'col'))
- grad_items: float32 [32768, 256], P(('col', 'row'))
The draws below stay inside these ranges and needn't reach their ends.
Inputs may be any that keep to these rules, and one draw needn't show every extreme that they name: `tile_count`: every cell has between 1 and 4 live slots, and some cell has all 4 live. `tile_pos`: the 4 positions of one cell are distinct numbers of 0 to 31; only the live ones count. `user_ids`: the triplets of the device at mesh index (r, c) name only that device's users, rows (r * 16 + c) * 64 to (r * 16 + c + 1) * 64 - 1. `pos_ids`: the triplets of the device at mesh index (r, c) name only that device's items, rows (c * 32 + r) * 64 to (c * 32 + r + 1) * 64 - 1. `neg_ids`: like pos_ids, and never equal to the same triplet's positive item.
All inputs are finite; a program needn't handle non-finite values.
Results may differ from the reference program's by a relative error of at most 0.003.
Values may be sent and summed in bfloat16 or wider, within the bound.
A program may use at most 64 MiB of HBM per device.

```python
import jax
import jax.numpy as jnp
from jax import lax

D = 256
TILE = 256
RB = 4
CB = 8
SLOTS = 4
BATCH_DEV = 256
GRID_ROWS = 32
GRID_COLS = 16
USR_DEV = 64
ITM_DEV = 64
NU = 32768
NI = 32768


def triplet_owner():
    total = BATCH_DEV * GRID_ROWS * GRID_COLS
    device_flat = jnp.arange(total, dtype=jnp.int32) // BATCH_DEV
    grid_row = device_flat // GRID_COLS
    grid_col = device_flat % GRID_COLS
    return (device_flat, grid_col * GRID_ROWS + grid_row)


def shared_positive(key):
    total = BATCH_DEV * GRID_ROWS * GRID_COLS
    positive = jax.random.randint(jax.random.fold_in(key, 5), (total,), 0, ITM_DEV, dtype=jnp.int32)
    positive = positive.at[0].set(0).at[1].set(1)
    positive = positive.at[total - 2].set(0).at[total - 1].set(ITM_DEV - 1)
    return positive


def draw_tile_count(key, part):
    key = jax.random.fold_in(key, 3)
    first_key, second_key = jax.random.split(key)
    raw_draw = jax.random.randint(first_key, (GRID_ROWS * GRID_COLS,), 0, SLOTS, dtype=jnp.int32)
    counts = 1 + raw_draw * raw_draw // (SLOTS - 1)
    busiest = jax.random.randint(second_key, (), 0, GRID_ROWS * GRID_COLS, dtype=jnp.int32)
    counts = counts.at[busiest].set(SLOTS)
    return counts.reshape(GRID_ROWS, GRID_COLS).astype(jnp.int32)


def draw_tile_pos(key, part):
    key = jax.random.fold_in(key, 7)
    scores = jax.random.randint(key, (GRID_ROWS, GRID_COLS, RB * CB), 0, 65536, dtype=jnp.int32)
    scores = scores * (RB * CB) + jnp.arange(RB * CB, dtype=jnp.int32)
    scores = scores.at[0, 0, 0].set(-2).at[0, 0, RB * CB - 1].set(-1)
    return jnp.argsort(scores, axis=-1)[:, :, :SLOTS].astype(jnp.int32)


def draw_user_ids(key, part):
    key = jax.random.fold_in(key, 11)
    device_flat, item_shard = triplet_owner()
    total = device_flat.shape[0]
    offsets = jax.random.randint(key, device_flat.shape, 0, USR_DEV, dtype=jnp.int32)
    offsets = offsets.at[0].set(0).at[total - 1].set(USR_DEV - 1)
    return (device_flat * USR_DEV + offsets).astype(jnp.int32)


def draw_pos_ids(key, part):
    positive = shared_positive(key)
    device_flat, item_shard = triplet_owner()
    return (item_shard * ITM_DEV + positive).astype(jnp.int32)


def draw_neg_ids(key, part):
    positive = shared_positive(key)
    key = jax.random.fold_in(key, 17)
    device_flat, item_shard = triplet_owner()
    total = positive.shape[0]
    offsets = jax.random.randint(key, positive.shape, 1, ITM_DEV, dtype=jnp.int32)
    offsets = offsets.at[1].set(ITM_DEV - 1).at[total - 2].set(ITM_DEV - 1)
    return (item_shard * ITM_DEV + (positive + offsets) % ITM_DEV).astype(jnp.int32)


def shard_levels(stream_key, shape, cuts, low, largest):
    gain = 1.0
    for position, shards_of in cuts:
        heights = jax.random.uniform(jax.random.fold_in(jax.random.fold_in(stream_key, 6), position), (shards_of,), jnp.float32, low / len(cuts), largest / len(cuts))
        gain = gain * jnp.repeat(jnp.exp(heights), shape[position] // shards_of).reshape((-1,) + (1,) * (len(shape) - 1 - position))
    return gain


def bell_draw(own_key, shape, width, limit, pieces=(), held_as=jnp.bfloat16):
    result = width * jax.random.normal(own_key, shape, jnp.float32)
    if pieces:
        result = result * shard_levels(own_key, shape, pieces, -0.22, 0.18)
    return jnp.clip(result, -limit, limit).astype(held_as)


def setup_inputs(seed: int = 0) -> dict:
    seeds = jax.random.split(jax.random.key(seed), 9)
    users = bell_draw(seeds[0], (NU, D), 1.0, 6.0, ((0, 512),), jnp.float32)
    items = bell_draw(seeds[1], (NI, D), 0.125, 0.75, ((0, 512),), jnp.float32)
    tiles = bell_draw(seeds[2], (GRID_ROWS, GRID_COLS, SLOTS, TILE, TILE), NI ** -0.5, 0.03125, ((0, 32), (1, 16)))
    tile_pos = draw_tile_pos(jax.random.fold_in(seeds[8], 71), 0)
    tile_count = draw_tile_count(jax.random.fold_in(seeds[8], 71), 0)
    user_ids = draw_user_ids(jax.random.fold_in(seeds[8], 71), 0)
    pos_ids = draw_pos_ids(jax.random.fold_in(seeds[8], 71), 0)
    neg_ids = draw_neg_ids(jax.random.fold_in(seeds[8], 71), 0)
    return {"users": users, "items": items, "tiles": tiles, "tile_pos": tile_pos, "tile_count": tile_count, "user_ids": user_ids, "pos_ids": pos_ids, "neg_ids": neg_ids}


def propagate(user_side, item_side, tiles, tile_pos, tile_count):
    user_tiles = user_side.reshape(GRID_ROWS * RB, TILE, D)
    item_tiles = item_side.reshape(GRID_COLS * CB, TILE, D)

    def visit(carry, flat_index):
        to_users, to_items = carry
        grid_row = flat_index // (GRID_COLS * SLOTS)
        grid_col = (flat_index // SLOTS) % GRID_COLS
        slot_index = flat_index % SLOTS
        weights = tiles[grid_row, grid_col, slot_index]
        placed = tile_pos[grid_row, grid_col, slot_index]
        live = slot_index < tile_count[grid_row, grid_col]
        user_tile = grid_row * RB + placed // CB
        item_tile = grid_col * CB + placed % CB
        into_users = jnp.dot(weights, item_tiles[item_tile], preferred_element_type=jnp.float32)
        into_items = jnp.dot(weights.T, user_tiles[user_tile], preferred_element_type=jnp.float32)
        into_users = jnp.where(live, into_users, jnp.zeros_like(into_users))
        into_items = jnp.where(live, into_items, jnp.zeros_like(into_items))
        return (to_users.at[user_tile].add(into_users), to_items.at[item_tile].add(into_items)), None

    start = (jnp.zeros((GRID_ROWS * RB, TILE, D), jnp.float32), jnp.zeros((GRID_COLS * CB, TILE, D), jnp.float32))
    totals, unused = lax.scan(visit, start, jnp.arange(GRID_ROWS * GRID_COLS * SLOTS, dtype=jnp.int32))
    return totals[0].reshape(NU, D), totals[1].reshape(NI, D)


def reference(users, items, tiles, tile_pos, tile_count, user_ids, pos_ids, neg_ids):
    first_users, first_items = propagate(users.astype(jnp.bfloat16), items.astype(jnp.bfloat16), tiles, tile_pos, tile_count)
    final_users = 0.5 * (users + first_users)
    final_items = 0.5 * (items + first_items)
    chosen = final_users[user_ids]
    contrast = final_items[pos_ids] - final_items[neg_ids]
    score = jnp.sum(chosen * contrast, axis=1)
    back = jax.nn.sigmoid(-score)[:, None]
    grad_final_users = jnp.zeros((NU, D), jnp.float32).at[user_ids].add(-back * contrast)
    grad_final_items = jnp.zeros((NI, D), jnp.float32).at[pos_ids].add(-back * chosen).at[neg_ids].add(back * chosen)
    back_users, back_items = propagate(grad_final_users.astype(jnp.bfloat16), grad_final_items.astype(jnp.bfloat16), tiles, tile_pos, tile_count)
    return 0.5 * grad_final_users + 0.5 * back_users, 0.5 * grad_final_items + 0.5 * back_items
```

```python
import functools

import jax
import jax.numpy as jnp
from jax import lax
from jax.experimental import pallas as pl
from jax.experimental.pallas import tpu as pltpu
from jax.sharding import PartitionSpec as P

MESH = pl.DeviceIdType.MESH
BF16 = jnp.bfloat16
F32 = jnp.float32
SLOTS = 4
ROWS = 64
WIDTH = 256
TILE = 256
USER_BLOCKS = 16
ITEM_GROUPS = 16
ITEM_TILES = 8


def masks_of(pos_ref, count_ref):
    filled = count_ref[0, 0]
    masks = []
    for slot in range(SLOTS):
        placed = pos_ref[0, slot]
        live = jnp.full((1, WIDTH), slot, jnp.int32) < jnp.full((1, WIDTH), filled, jnp.int32)
        wide = jnp.full((1, WIDTH), placed, jnp.int32)
        masks.append(
            (placed >> 3, placed & 7, jnp.where(live, wide >> 3, -1), jnp.where(live, wide & 7, -1))
        )
    return masks


def pick(masks, which, index):
    return [jnp.where(mask[2 + which] == index, 1.0, 0.0).astype(F32) for mask in masks]


def kernel(
    users_ref,
    items_ref,
    pos_ref,
    count_ref,
    uid_ref,
    pid_ref,
    nid_ref,
    tiles_hbm,
    out_users_ref,
    out_items_ref,
    tiles,
    tiles_t,
    user_panel_0,
    user_panel_1,
    item_panel_0,
    item_panel_1,
    prod_users,
    prod_items,
    sum_users,
    sum_items,
    mate_items,
    pair_items,
    recv_users,
    recv_items,
    load_sem,
    gu_send,
    gu_recv,
    gi_send,
    gi_recv,
    mi_send,
    mi_recv,
    rm_send,
    rm_recv,
    ru_send,
    ru_recv,
    ri_send,
    ri_recv,
):
    row = lax.axis_index("row")
    col = lax.axis_index("col")
    core = lax.rem(row, 2)
    group = row // 2
    mate = (row + 1 - 2 * core, col)

    def user_peer(step):
        return (row, lax.rem(col + step, USER_BLOCKS))

    def item_peer(step):
        return (lax.rem(group + step, ITEM_GROUPS) * 2 + core, col)

    load = pltpu.make_async_copy(tiles_hbm, tiles, load_sem)
    load.start()

    barrier = pltpu.get_barrier_semaphore()
    for step in range(1, USER_BLOCKS):
        pl.semaphore_signal(barrier, 1, device_id=user_peer(step), device_id_type=MESH)
        pl.semaphore_signal(barrier, 1, device_id=item_peer(step), device_id_type=MESH)
    pl.semaphore_signal(barrier, 1, device_id=mate, device_id_type=MESH)
    pl.semaphore_wait(barrier, 2 * (USER_BLOCKS - 1) + 1)

    masks = masks_of(pos_ref, count_ref)
    user_panel = (user_panel_0, user_panel_1)
    item_panel = (item_panel_0, item_panel_1)

    def block_of(panel, position):
        return panel.at[position // 4, lax.rem(position, 4)]

    def gather_users(turn, own):
        panel = user_panel[turn]
        block_of(panel, col)[...] = own
        for step in range(1, USER_BLOCKS):
            pltpu.make_async_remote_copy(
                src_ref=block_of(panel, col),
                dst_ref=block_of(panel, col),
                send_sem=gu_send.at[turn],
                recv_sem=gu_recv.at[turn],
                device_id=user_peer(step),
                device_id_type=MESH,
            ).start()

    def item_copy(turn, which_row, step, device):
        panel = item_panel[turn]
        return pltpu.make_async_remote_copy(
            src_ref=block_of(panel, which_row),
            dst_ref=block_of(panel, which_row),
            send_sem=gi_send.at[turn],
            recv_sem=gi_recv.at[turn, step],
            device_id=device,
            device_id_type=MESH,
        )

    def mate_copy(turn, which_row):
        panel = item_panel[turn]
        return pltpu.make_async_remote_copy(
            src_ref=block_of(panel, which_row),
            dst_ref=block_of(panel, which_row),
            send_sem=mi_send.at[turn],
            recv_sem=mi_recv.at[turn],
            device_id=mate,
            device_id_type=MESH,
        )

    def gather_items(turn, own):
        panel = item_panel[turn]
        block_of(panel, row)[...] = own
        for step in range(1, ITEM_GROUPS):
            item_copy(turn, row, step, item_peer(step)).start()
        mate_copy(turn, row).start()

    def bulk_wait(ref, send_sem, recv_sem, send):
        copy = pltpu.make_async_remote_copy(
            src_ref=ref, dst_ref=ref, send_sem=send_sem, recv_sem=recv_sem,
            device_id=mate, device_id_type=MESH,
        )
        if send:
            copy.wait_send()
        else:
            copy.wait_recv()

    def relay_items(turn):
        for step in range(1, ITEM_GROUPS):
            source = lax.rem(group + ITEM_GROUPS - step, ITEM_GROUPS) * 2 + core
            item_copy(turn, source, step, mate).wait_recv()
            mate_copy(turn, source).start()
        half = item_panel[turn].at[pl.ds(0, 4)]
        bulk_wait(half, mi_send.at[turn], mi_recv.at[turn], False)

    def spread(turn):
        for slot in range(SLOTS):
            placed = item_panel[turn][masks[slot][1]].reshape(TILE, WIDTH)
            prod_users[slot] = jnp.dot(tiles[slot], placed, preferred_element_type=F32)

        def add_users(block, carry):
            weights = pick(masks, 0, block // 4)
            rows = pl.ds(pl.multiple_of(lax.rem(block, 4) * ROWS, ROWS), ROWS)
            total = weights[0] * prod_users[0, rows, :]
            for slot in range(1, SLOTS):
                total += weights[slot] * prod_users[slot, rows, :]
            sum_users[turn, block] = total.astype(BF16)
            return carry

        lax.fori_loop(0, USER_BLOCKS, add_users, 0)
        for step in range(1, USER_BLOCKS):
            pltpu.make_async_remote_copy(
                src_ref=sum_users.at[turn, lax.rem(col + step, USER_BLOCKS)],
                dst_ref=recv_users.at[turn, step],
                send_sem=ru_send.at[turn],
                recv_sem=ru_recv.at[turn],
                device_id=user_peer(step),
                device_id_type=MESH,
            ).start()

    def spread_items(turn):
        for slot in range(SLOTS):
            placed = user_panel[turn][masks[slot][0]].reshape(TILE, WIDTH)
            prod_items[slot] = jnp.dot(tiles_t[slot], placed, preferred_element_type=F32)

        def add_items(block, carry):
            weights = pick(masks, 1, block // 4)
            rows = pl.ds(pl.multiple_of(lax.rem(block, 4) * ROWS, ROWS), ROWS)
            total = weights[0] * prod_items[0, rows, :]
            for slot in range(1, SLOTS):
                total += weights[slot] * prod_items[slot, rows, :]
            sum_items[turn, lax.rem(block, 2), block // 2] = total.astype(BF16)
            return carry

        lax.fori_loop(0, 2 * ITEM_GROUPS, add_items, 0)
        pltpu.make_async_remote_copy(
            src_ref=sum_items.at[turn, 1 - core],
            dst_ref=mate_items.at[turn],
            send_sem=rm_send.at[turn],
            recv_sem=rm_recv.at[turn],
            device_id=mate,
            device_id_type=MESH,
        ).start()

    def pair_up(turn):
        bulk_wait(mate_items.at[turn], rm_send.at[turn], rm_recv.at[turn], False)

        def add_pair(block, carry):
            pair_items[turn, block] = (
                sum_items[turn, core, block].astype(F32) + mate_items[turn, block].astype(F32)
            ).astype(BF16)
            return carry

        lax.fori_loop(0, ITEM_GROUPS, add_pair, 0)
        for step in range(1, ITEM_GROUPS):
            pltpu.make_async_remote_copy(
                src_ref=pair_items.at[turn, lax.rem(group + step, ITEM_GROUPS)],
                dst_ref=recv_items.at[turn, step],
                send_sem=ri_send.at[turn],
                recv_sem=ri_recv.at[turn],
                device_id=item_peer(step),
                device_id_type=MESH,
            ).start()

    def total_of(own, received):
        total = own.astype(F32)
        for step in range(1, USER_BLOCKS):
            total += received[step].astype(F32)
        return total

    def propagate(turn, own_users, own_items):
        gather_items(turn, own_items)
        gather_users(turn, own_users)
        if turn == 0:
            load.wait()
            for slot in range(SLOTS):
                tiles_t[slot] = tiles[slot].T
        bulk_wait(
            recv_users.at[turn, pl.ds(1, USER_BLOCKS - 1)],
            gu_send.at[turn], gu_recv.at[turn], False,
        )
        spread_items(turn)
        relay_items(turn)
        spread(turn)
        pair_up(turn)
        first = pl.ds(1, USER_BLOCKS - 1)
        bulk_wait(recv_users.at[turn, first], ru_send.at[turn], ru_recv.at[turn], False)
        to_users = total_of(sum_users[turn, col], recv_users.at[turn])
        bulk_wait(recv_items.at[turn, first], ri_send.at[turn], ri_recv.at[turn], False)
        to_items = total_of(pair_items[turn, group], recv_items.at[turn])
        return to_users, to_items

    first_users, first_items = propagate(
        0, users_ref[...].astype(BF16), items_ref[...].astype(BF16)
    )
    final_users = 0.5 * (users_ref[...] + first_users)
    final_items = 0.5 * (items_ref[...] + first_items)

    user_base = (row * USER_BLOCKS + col) * ROWS
    item_base = (col * 2 * ITEM_GROUPS + row) * ROWS
    batch = uid_ref.shape[1]
    places = lax.broadcasted_iota(jnp.int32, (ROWS, batch), 0)
    user_hot = jnp.where(places == uid_ref[...] - user_base, 1.0, 0.0).astype(F32)
    item_hot = jnp.where(places == nid_ref[...] - item_base, 1.0, 0.0).astype(F32)
    item_hot = item_hot - jnp.where(places == pid_ref[...] - item_base, 1.0, 0.0).astype(F32)
    dot = functools.partial(
        jnp.dot, precision=lax.Precision.HIGHEST, preferred_element_type=F32
    )
    chosen = dot(user_hot.T, final_users)
    against = dot(item_hot.T, final_items)
    score = -jnp.sum(chosen * against, axis=1, keepdims=True)
    back = jax.nn.sigmoid(-score)
    grad_users = dot(user_hot, back * against)
    grad_items = dot(item_hot, back * chosen)

    back_users, back_items = propagate(1, grad_users.astype(BF16), grad_items.astype(BF16))
    out_users_ref[...] = 0.5 * grad_users + 0.5 * back_users
    out_items_ref[...] = 0.5 * grad_items + 0.5 * back_items

    for turn in range(2):
        first = pl.ds(1, USER_BLOCKS - 1)
        bulk_wait(recv_users.at[turn, first], gu_send.at[turn], gu_recv.at[turn], True)
        bulk_wait(recv_items.at[turn, first], gi_send.at[turn], gi_recv.at[turn, 0], True)
        half = item_panel[turn].at[pl.ds(0, 4)]
        bulk_wait(half, mi_send.at[turn], mi_recv.at[turn], True)
        bulk_wait(mate_items.at[turn], rm_send.at[turn], rm_recv.at[turn], True)
        bulk_wait(recv_users.at[turn, first], ru_send.at[turn], ru_recv.at[turn], True)
        bulk_wait(recv_items.at[turn, first], ri_send.at[turn], ri_recv.at[turn], True)


def on_device(users, items, tiles, tile_pos, tile_count, user_ids, pos_ids, neg_ids):
    vmem = pl.BlockSpec(memory_space=pltpu.VMEM)
    smem = pl.BlockSpec(memory_space=pltpu.SMEM)
    dma = pltpu.SemaphoreType.DMA
    batch = user_ids.shape[0]
    return pl.pallas_call(
        kernel,
        out_shape=(
            jax.ShapeDtypeStruct((ROWS, WIDTH), F32),
            jax.ShapeDtypeStruct((ROWS, WIDTH), F32),
        ),
        in_specs=[vmem, vmem, smem, smem, vmem, vmem, vmem, pl.BlockSpec(memory_space=pl.ANY)],
        out_specs=(vmem, vmem),
        scratch_shapes=[
            pltpu.VMEM((SLOTS, TILE, TILE), BF16),
            pltpu.VMEM((SLOTS, TILE, TILE), BF16),
            pltpu.VMEM((4, 4, ROWS, WIDTH), BF16),
            pltpu.VMEM((4, 4, ROWS, WIDTH), BF16),
            pltpu.VMEM((ITEM_TILES, 4, ROWS, WIDTH), BF16),
            pltpu.VMEM((ITEM_TILES, 4, ROWS, WIDTH), BF16),
            pltpu.VMEM((SLOTS, TILE, WIDTH), F32),
            pltpu.VMEM((SLOTS, TILE, WIDTH), F32),
            pltpu.VMEM((2, USER_BLOCKS, ROWS, WIDTH), BF16),
            pltpu.VMEM((2, 2, ITEM_GROUPS, ROWS, WIDTH), BF16),
            pltpu.VMEM((2, ITEM_GROUPS, ROWS, WIDTH), BF16),
            pltpu.VMEM((2, ITEM_GROUPS, ROWS, WIDTH), BF16),
            pltpu.VMEM((2, USER_BLOCKS, ROWS, WIDTH), BF16),
            pltpu.VMEM((2, ITEM_GROUPS, ROWS, WIDTH), BF16),
            dma,
            dma((2,)),
            dma((2,)),
            dma((2,)),
            dma((2, ITEM_GROUPS)),
            dma((2,)),
            dma((2,)),
            dma((2,)),
            dma((2,)),
            dma((2,)),
            dma((2,)),
            dma((2,)),
            dma((2,)),
        ],
        compiler_params=pltpu.CompilerParams(
            collective_id=0, has_side_effects=True, vmem_limit_bytes=40 << 20
        ),
        name="propagation_layer",
    )(
        users,
        items,
        tile_pos.reshape(1, SLOTS),
        tile_count,
        user_ids.reshape(1, batch),
        pos_ids.reshape(1, batch),
        neg_ids.reshape(1, batch),
        tiles.reshape(SLOTS, TILE, TILE),
    )


def solution(mesh):
    placed = (
        P(("row", "col"), None),
        P(("col", "row"), None),
        P("row", "col", None, None, None),
        P("row", "col", None),
        P("row", "col"),
        P(("row", "col")),
        P(("row", "col")),
        P(("row", "col")),
    )
    return jax.shard_map(
        on_device,
        mesh=mesh,
        in_specs=placed,
        out_specs=(P(("row", "col"), None), P(("col", "row"), None)),
        check_vma=False,
    )
```

```python
import functools

import jax
import jax.numpy as jnp
from jax import lax
from jax.experimental import pallas as pl
from jax.experimental.pallas import tpu as pltpu
from jax.sharding import PartitionSpec as P

MESH = pl.DeviceIdType.MESH
BF16 = jnp.bfloat16
F32 = jnp.float32
SLOTS = 4
ROWS = 64
HALF = 128
WIDTH = 256
TILE = 256
RING = 8
BLOCKS = 16
USERS, ITEMS = 0, 1


def split(value, parts):
    terms = []
    for part in range(parts):
        term = value.astype(BF16)
        terms.append(term)
        value = value - term.astype(F32)
    return jnp.concatenate(terms, axis=0)


def kernel(
    users_ref,
    items_ref,
    pos_ref,
    count_ref,
    uid_ref,
    pid_ref,
    nid_ref,
    tiles_hbm,
    out_users_ref,
    out_items_ref,
    tiles,
    tiles_t,
    meta,
    meta_smem,
    user_hot,
    item_hot,
    user_hot_t,
    item_hot_t,
    user_panel_0,
    user_panel_1,
    item_panel_0,
    item_panel_1,
    stage,
    prod,
    sums,
    far,
    relayed,
    near,
    x_out,
    x_in,
    pair_sum,
    halves,
    load_sem,
    tile_send,
    tile_recv,
    meta_sem,
    meta_send,
    meta_recv,
    gm_send,
    gm_recv,
    gx_recv,
    g2_recv,
    gb_send,
    gb_recv,
    sf_recv,
    sn_recv,
    s_send,
    sx_send,
    sx_recv,
    sm_send,
    sm_recv,
):
    row = lax.axis_index("row")
    col = lax.axis_index("col")
    core = lax.rem(row, 2)
    group = row // 2
    mate = (row + 1 - 2 * core, col)
    x_at = (col // RING, group // RING)
    ring_at = (lax.rem(col, RING), lax.rem(group, RING))

    def device(which, x, ring):
        if which == USERS:
            return (row, x * RING + ring)
        return ((x * RING + ring) * 2 + core, col)

    def along(which, step):
        return device(which, x_at[which], lax.rem(ring_at[which] + step + RING, RING))

    def across(which):
        return device(which, 1 - x_at[which], ring_at[which])

    def block(which, other, step):
        x = 1 - x_at[which] if other else x_at[which]
        return x * RING + lax.rem(ring_at[which] + step + RING, RING)

    def send(source, target, send_sem, recv_sem, to):
        pltpu.make_async_remote_copy(
            src_ref=source, dst_ref=target, send_sem=send_sem, recv_sem=recv_sem,
            device_id=to, device_id_type=MESH,
        ).start()

    def awaits(ref, sem):
        pltpu.make_async_remote_copy(
            src_ref=ref, dst_ref=ref, send_sem=sem, recv_sem=sem,
            device_id=mate, device_id_type=MESH,
        ).wait_recv()

    def sent(ref, sem):
        pltpu.make_async_remote_copy(
            src_ref=ref, dst_ref=ref, send_sem=sem, recv_sem=sem,
            device_id=mate, device_id_type=MESH,
        ).wait_send()

    barrier = pltpu.get_barrier_semaphore()
    peers = [mate]
    for which in (USERS, ITEMS):
        peers += [across(which)] + [along(which, step) for step in (1, -1, 2, -2)]
    for peer in peers:
        pl.semaphore_signal(barrier, 1, device_id=peer, device_id_type=MESH)

    load = pltpu.make_async_copy(tiles_hbm, tiles.at[core], load_sem)
    load.start()
    filled = jnp.full((8, HALF), count_ref[0, 0], jnp.int32)
    slot_of = lax.broadcasted_iota(jnp.int32, (8, HALF), 0)
    placed = jnp.full((8, HALF), pos_ref[0, 0], jnp.int32)
    for slot in range(1, SLOTS):
        placed = jnp.where(slot_of == slot, jnp.full((8, HALF), pos_ref[0, slot], jnp.int32), placed)
    meta[core] = jnp.where(slot_of < filled, placed, placed + 64)

    panels = ((user_panel_0, item_panel_0), (user_panel_1, item_panel_1))

    def at_block(turn, which, number):
        per = 4 if which == USERS else 2
        return panels[turn][which].at[number // per, lax.rem(number, per)]

    def own_rows(turn, which, value):
        stage[turn, which, 0] = value[:, :HALF].astype(BF16)
        stage[turn, which, 1] = value[:, HALF:].astype(BF16)
        own = at_block(turn, which, block(which, False, 0))
        own[core] = stage[turn, which, core]

    def gather_mate(turn, which):
        own = at_block(turn, which, block(which, False, 0))
        send(stage.at[turn, which, 1 - core], own.at[core],
             gm_send.at[turn, which], gm_recv.at[turn, which], mate)

    def gather_block(turn, which, other):
        here = at_block(turn, which, block(which, other, 0))
        for step in (2, -2):
            send(here, here, gb_send.at[turn, which],
                 g2_recv.at[turn, which, int(other), int(step < 0)], along(which, step))
        for step in (1, -1):
            send(here, here, gb_send.at[turn, which], gb_recv.at[turn, which], along(which, step))

    def gather_own(turn, which):
        own = at_block(turn, which, block(which, False, 0))
        awaits(own.at[1 - core], gm_recv.at[turn, which])
        send(own, own, gb_send.at[turn, which], gx_recv.at[turn, which], across(which))
        gather_block(turn, which, False)

    def gather_across(turn, which):
        awaits(at_block(turn, which, block(which, True, 0)), gx_recv.at[turn, which])
        gather_block(turn, which, True)

    def gather_relay(turn, which, other):
        for way, step in ((0, 1), (1, -1)):
            here = at_block(turn, which, block(which, other, -2 * step))
            awaits(here, g2_recv.at[turn, which, int(other), way])
            part = here.at[way]
            send(part, part, gb_send.at[turn, which], gb_recv.at[turn, which], along(which, 2 * step))
            send(here, here, gb_send.at[turn, which], gb_recv.at[turn, which], along(which, step))

    def gather_end(turn, which):
        awaits(sums.at[turn, which, pl.ds(0, 10)], gb_recv.at[turn, which])

    def marks(cell, slot):
        return meta[cell, pl.ds(slot, 1), :]

    def spread_users(turn):
        panel = panels[turn][ITEMS]
        for cell in range(2):
            for slot in range(SLOTS):
                rows = panel[meta_smem[cell, slot, 0] & 7].reshape(TILE, HALF)
                prod[cell * SLOTS + slot] = jnp.dot(
                    tiles[cell, slot], rows, preferred_element_type=F32
                )

        def add(number, carry):
            start = pl.ds(pl.multiple_of(lax.rem(number, 4) * ROWS, ROWS), ROWS)
            for cell in range(2):
                total = jnp.zeros((ROWS, HALF), F32)
                for slot in range(SLOTS):
                    weight = jnp.where((marks(cell, slot) >> 3) == number // 4, 1.0, 0.0)
                    total += weight.astype(F32) * prod[cell * SLOTS + slot, start, :]
                sums[turn, USERS, number, cell] = total.astype(BF16)
            return carry

        lax.fori_loop(0, BLOCKS, add, 0)

    def spread_items(turn):
        panel = panels[turn][USERS]
        for cell in range(2):
            for slot in range(SLOTS):
                tile = (meta_smem[cell, slot, 0] >> 3) & 3
                rows = panel[tile, :, cell].reshape(TILE, HALF)
                prod[cell * SLOTS + slot] = jnp.dot(
                    tiles_t[cell, slot], rows, preferred_element_type=F32
                )

        def add(number, carry):
            for owner in range(2):
                start = (lax.rem(number, 2) * 2 + owner) * ROWS
                start = pl.ds(pl.multiple_of(start, ROWS), ROWS)
                total = jnp.zeros((ROWS, HALF), F32)
                for cell in range(2):
                    for slot in range(SLOTS):
                        weight = jnp.where((marks(cell, slot) & 71) == number // 2, 1.0, 0.0)
                        total += weight.astype(F32) * prod[cell * SLOTS + slot, start, :]
                sums[turn, ITEMS, number, owner] = total.astype(BF16)
            return carry

        lax.fori_loop(0, BLOCKS, add, 0)

    def scatter_start(turn, which):
        out = s_send.at[turn, which]
        for other in (True, False):
            e = int(other)
            for way, step in ((0, 1), (1, -1)):
                sem = sf_recv.at[turn, which, e, way]
                send(sums.at[turn, which, block(which, other, 4), way],
                     far.at[turn, which, e, way, 2], out, sem, along(which, 2 * step))
                send(sums.at[turn, which, block(which, other, 3 * step)],
                     far.at[turn, which, e, way, pl.ds(0, 2)], out, sem, along(which, step))
        for other in (True, False):
            e = int(other)
            for way, step in ((0, 1), (1, -1)):
                send(sums.at[turn, which, block(which, other, step)],
                     near.at[turn, which, e, way], out, sn_recv.at[turn, which, e], along(which, step))

    def scatter_relay(turn, which, other):
        e = int(other)
        for way, step in ((0, 1), (1, -1)):
            came = far.at[turn, which, e, way]
            awaits(came, sf_recv.at[turn, which, e, way])
            mine = sums.at[turn, which, block(which, other, 2 * step)]
            for owner in range(2):
                total = mine[owner].astype(F32) + came[owner].astype(F32)
                if owner == way:
                    total += came[2].astype(F32)
                relayed[turn, which, e, way, owner] = total.astype(BF16)
            send(relayed.at[turn, which, e, way], near.at[turn, which, e, 2 + way],
                 s_send.at[turn, which], sn_recv.at[turn, which, e], along(which, 2 * step))

    def scatter_sum(turn, which, other):
        e = int(other)
        awaits(near.at[turn, which, e], sn_recv.at[turn, which, e])
        into = x_out.at[turn, which] if other else pair_sum.at[turn, which]
        for owner in range(2):
            total = sums[turn, which, block(which, other, 0), owner].astype(F32)
            for part in range(4):
                total += near[turn, which, e, part, owner].astype(F32)
            into[owner] = total
        if other:
            send(x_out.at[turn, which], x_in.at[turn, which],
                 sx_send.at[turn, which], sx_recv.at[turn, which], across(which))

    def scatter_pair(turn, which):
        awaits(x_in.at[turn, which], sx_recv.at[turn, which])
        for owner in range(2):
            pair_sum[turn, which, owner] += x_in[turn, which, owner]
        send(pair_sum.at[turn, which, 1 - core], halves.at[turn, which, core],
             sm_send.at[turn, which], sm_recv.at[turn, which], mate)
        halves[turn, which, core] = pair_sum[turn, which, core]

    def scatter_end(turn, which):
        awaits(halves.at[turn, which, 1 - core], sm_recv.at[turn, which])
        return jnp.concatenate([halves[turn, which, 0], halves[turn, which, 1]], axis=1)

    def prepare():
        user_base = (row * BLOCKS + col) * ROWS
        item_base = (col * 2 * BLOCKS + row) * ROWS
        places = lax.broadcasted_iota(jnp.int32, (ROWS, uid_ref.shape[1]), 0)
        hot = jnp.where(places == uid_ref[...] - user_base, 1.0, 0.0).astype(F32)
        user_hot[...] = hot.astype(BF16)
        user_hot_t[...] = jnp.concatenate([hot] * 3, axis=0).T.astype(BF16)
        hot = jnp.where(places == nid_ref[...] - item_base, 1.0, 0.0).astype(F32)
        hot = hot - jnp.where(places == pid_ref[...] - item_base, 1.0, 0.0).astype(F32)
        item_hot[...] = hot.astype(BF16)
        item_hot_t[...] = jnp.concatenate([hot] * 3, axis=0).T.astype(BF16)

    both = (ITEMS, USERS)

    def propagate(turn):
        for which in both:
            gather_mate(turn, which)
        if turn == 0:
            send(tiles_hbm, tiles.at[core], tile_send, tile_recv, mate)
            send(meta.at[core], meta.at[core], meta_send, meta_recv, mate)
        for which in both:
            gather_own(turn, which)
        if turn == 0:
            prepare()
        for which in both:
            gather_across(turn, which)
        for which in both:
            gather_relay(turn, which, False)
        if turn == 0:
            load.wait()
            awaits(meta.at[1 - core], meta_recv)
            fill = pltpu.make_async_copy(meta, meta_smem, meta_sem)
            fill.start()
            fill.wait()
        for which in both:
            gather_relay(turn, which, True)
        if turn == 0:
            awaits(tiles.at[1 - core], tile_recv)
            for cell in range(2):
                for slot in range(SLOTS):
                    tiles_t[cell, slot] = tiles[cell, slot].T
        gather_end(turn, ITEMS)
        spread_users(turn)
        scatter_start(turn, USERS)
        gather_end(turn, USERS)
        spread_items(turn)
        scatter_start(turn, ITEMS)
        for other in (True, False):
            for which in (USERS, ITEMS):
                scatter_relay(turn, which, other)
        for other in (True, False):
            for which in (USERS, ITEMS):
                scatter_sum(turn, which, other)
        for which in (USERS, ITEMS):
            scatter_pair(turn, which)
        return scatter_end(turn, USERS), scatter_end(turn, ITEMS)

    own_rows(0, ITEMS, items_ref[...])
    own_rows(0, USERS, users_ref[...])
    pl.semaphore_wait(barrier, len(peers))
    first_users, first_items = propagate(0)
    final_users = 0.5 * (users_ref[...] + first_users)
    final_items = 0.5 * (items_ref[...] + first_items)

    dot = functools.partial(jnp.dot, preferred_element_type=F32)
    chosen = dot(user_hot_t[...], split(final_users, 3))
    against = dot(item_hot_t[...], split(final_items, 3))
    score = -jnp.sum(chosen * against, axis=1, keepdims=True)
    back = jax.nn.sigmoid(-score)
    hot = user_hot[...]
    grad_users = dot(jnp.concatenate([hot] * 3, axis=1), split(back * against, 3))
    hot = item_hot[...]
    grad_items = dot(jnp.concatenate([hot] * 3, axis=1), split(back * chosen, 3))

    own_rows(1, ITEMS, grad_items)
    own_rows(1, USERS, grad_users)
    back_users, back_items = propagate(1)
    out_users_ref[...] = 0.5 * grad_users + 0.5 * back_users
    out_items_ref[...] = 0.5 * grad_items + 0.5 * back_items

    sent(tiles_hbm, tile_send)
    sent(meta.at[core], meta_send)
    for turn in range(2):
        for which in (USERS, ITEMS):
            sent(stage.at[turn, which, core], gm_send.at[turn, which])
            sent(sums.at[turn, which, pl.ds(0, 15)], gb_send.at[turn, which])
            sent(sums.at[turn, which, pl.ds(0, 14)], s_send.at[turn, which])
            sent(x_out.at[turn, which], sx_send.at[turn, which])
            sent(pair_sum.at[turn, which, core], sm_send.at[turn, which])


def on_device(users, items, tiles, tile_pos, tile_count, user_ids, pos_ids, neg_ids):
    vmem = pl.BlockSpec(memory_space=pltpu.VMEM)
    smem = pl.BlockSpec(memory_space=pltpu.SMEM)
    dma = pltpu.SemaphoreType.DMA
    batch = user_ids.shape[0]
    cut = (2, ROWS, HALF)
    return pl.pallas_call(
        kernel,
        out_shape=(
            jax.ShapeDtypeStruct((ROWS, WIDTH), F32),
            jax.ShapeDtypeStruct((ROWS, WIDTH), F32),
        ),
        in_specs=[vmem, vmem, smem, smem, vmem, vmem, vmem, pl.BlockSpec(memory_space=pl.ANY)],
        out_specs=(vmem, vmem),
        scratch_shapes=[
            pltpu.VMEM((2, SLOTS, TILE, TILE), BF16),
            pltpu.VMEM((2, SLOTS, TILE, TILE), BF16),
            pltpu.VMEM((2, 8, HALF), jnp.int32),
            pltpu.SMEM((2, 8, HALF), jnp.int32),
            pltpu.VMEM((ROWS, batch), BF16),
            pltpu.VMEM((ROWS, batch), BF16),
            pltpu.VMEM((batch, 3 * ROWS), BF16),
            pltpu.VMEM((batch, 3 * ROWS), BF16),
            pltpu.VMEM((4, 4) + cut, BF16),
            pltpu.VMEM((4, 4) + cut, BF16),
            pltpu.VMEM((8, 2) + cut, BF16),
            pltpu.VMEM((8, 2) + cut, BF16),
            pltpu.VMEM((2, 2) + cut, BF16),
            pltpu.VMEM((2 * SLOTS, TILE, HALF), F32),
            pltpu.VMEM((2, 2, BLOCKS) + cut, BF16),
            pltpu.VMEM((2, 2, 2, 2, 3, ROWS, HALF), BF16),
            pltpu.VMEM((2, 2, 2, 2) + cut, BF16),
            pltpu.VMEM((2, 2, 2, 4) + cut, BF16),
            pltpu.VMEM((2, 2) + cut, F32),
            pltpu.VMEM((2, 2) + cut, F32),
            pltpu.VMEM((2, 2) + cut, F32),
            pltpu.VMEM((2, 2) + cut, F32),
            dma,
            dma,
            dma,
            dma,
            dma,
            dma,
            dma((2, 2)),
            dma((2, 2)),
            dma((2, 2)),
            dma((2, 2, 2, 2)),
            dma((2, 2)),
            dma((2, 2)),
            dma((2, 2, 2, 2)),
            dma((2, 2, 2)),
            dma((2, 2)),
            dma((2, 2)),
            dma((2, 2)),
            dma((2, 2)),
            dma((2, 2)),
        ],
        compiler_params=pltpu.CompilerParams(
            collective_id=0, has_side_effects=True, vmem_limit_bytes=40 << 20
        ),
        name="propagation_layer",
    )(
        users,
        items,
        tile_pos.reshape(1, SLOTS),
        tile_count,
        user_ids.reshape(1, batch),
        pos_ids.reshape(1, batch),
        neg_ids.reshape(1, batch),
        tiles.reshape(SLOTS, TILE, TILE),
    )


def solution(mesh):
    placed = (
        P(("row", "col"), None),
        P(("col", "row"), None),
        P("row", "col", None, None, None),
        P("row", "col", None),
        P("row", "col"),
        P(("row", "col")),
        P(("row", "col")),
        P(("row", "col")),
    )
    return jax.shard_map(
        on_device,
        mesh=mesh,
        in_specs=placed,
        out_specs=(P(("row", "col"), None), P(("col", "row"), None)),
        check_vma=False,
    )
```

```python
import functools

import jax
import jax.numpy as jnp
from jax import lax
from jax.experimental import pallas as pl
from jax.experimental.pallas import tpu as pltpu
from jax.sharding import PartitionSpec as P

MESH = pl.DeviceIdType.MESH
BF16 = jnp.bfloat16
F32 = jnp.float32
SLOTS = 4
ROWS = 64
HALF = 128
WIDTH = 256
TILE = 256
RING = 8
BLOCKS = 16
USERS, ITEMS = 0, 1


def split(value, parts):
    terms = []
    for part in range(parts):
        term = value.astype(BF16)
        terms.append(term)
        value = value - term.astype(F32)
    return jnp.concatenate(terms, axis=0)


def kernel(
    users_hbm,
    items_hbm,
    pos_hbm,
    count_hbm,
    uid_hbm,
    pid_hbm,
    nid_hbm,
    tiles_hbm,
    out_users_ref,
    out_items_ref,
    users_ref,
    items_ref,
    pos_ref,
    count_ref,
    uid_ref,
    pid_ref,
    nid_ref,
    tiles,
    tiles_t,
    meta,
    meta_smem,
    user_hot,
    item_hot,
    user_hot_t,
    item_hot_t,
    user_panel_0,
    user_panel_1,
    item_panel_0,
    item_panel_1,
    stage,
    prod,
    sums,
    far,
    relayed,
    last,
    load_sem,
    tile_send,
    tile_recv,
    meta_sem,
    meta_send,
    meta_recv,
    gm_send,
    gm_recv,
    g2_recv,
    gb_send,
    gb_recv,
    sf_recv,
    sl_recv,
    s_send,
    sm_send,
):
    row = lax.axis_index("row")
    col = lax.axis_index("col")
    core = lax.rem(row, 2)
    group = row // 2
    mate = (row + 1 - 2 * core, col)
    x_at = (col // RING, group // RING)
    ring_at = (lax.rem(col, RING), lax.rem(group, RING))

    def block(which, other, step):
        x = 1 - x_at[which] if other else x_at[which]
        return x * RING + lax.rem(ring_at[which] + step + RING, RING)

    def device(which, other, step, to_core):
        number = block(which, other, step)
        if which == USERS:
            return (group * 2 + to_core, number)
        return (number * 2 + to_core, col)

    def along(which, step):
        return device(which, False, step, core)

    def send(source, target, send_sem, recv_sem, to):
        pltpu.make_async_remote_copy(
            src_ref=source, dst_ref=target, send_sem=send_sem, recv_sem=recv_sem,
            device_id=to, device_id_type=MESH,
        ).start()

    def awaits(ref, sem):
        pltpu.make_async_remote_copy(
            src_ref=ref, dst_ref=ref, send_sem=sem, recv_sem=sem,
            device_id=mate, device_id_type=MESH,
        ).wait_recv()

    def sent(ref, sem):
        pltpu.make_async_remote_copy(
            src_ref=ref, dst_ref=ref, send_sem=sem, recv_sem=sem,
            device_id=mate, device_id_type=MESH,
        ).wait_send()

    def load(number, source, target):
        copy = pltpu.make_async_copy(source, target, load_sem.at[number])
        copy.start()
        return copy

    items_load = load(0, items_hbm, items_ref)
    users_load = load(1, users_hbm, users_ref)
    pos_load = load(2, pos_hbm, pos_ref)
    count_load = load(3, count_hbm, count_ref)
    ids_load = [
        load(4, uid_hbm, uid_ref), load(5, pid_hbm, pid_ref), load(6, nid_hbm, nid_ref)
    ]
    tiles_load = load(7, tiles_hbm, tiles.at[core])

    barrier = pltpu.get_barrier_semaphore()
    far_steps = [(other, step) for step in (2, -2) for other in (True, False)]
    near_steps = [(other, step) for step in (1, -1) for other in (True, False)] + [(True, 0)]
    peers = [mate]
    for which in (USERS, ITEMS):
        for other, step in far_steps + near_steps:
            peers += [device(which, other, step, to_core) for to_core in range(2)]
    for peer in peers:
        pl.semaphore_signal(barrier, 1, device_id=peer, device_id_type=MESH)

    pos_load.wait()
    count_load.wait()
    filled = jnp.full((8, HALF), count_ref[0, 0], jnp.int32)
    slot_of = lax.broadcasted_iota(jnp.int32, (8, HALF), 0)
    placed = jnp.full((8, HALF), pos_ref[0, 0], jnp.int32)
    for slot in range(1, SLOTS):
        placed = jnp.where(slot_of == slot, jnp.full((8, HALF), pos_ref[0, slot], jnp.int32), placed)
    meta[core] = jnp.where(slot_of < filled, placed, placed + 64)

    panels = ((user_panel_0, item_panel_0), (user_panel_1, item_panel_1))

    def at_block(turn, which, number):
        per = 4 if which == USERS else 2
        return panels[turn][which].at[number // per, lax.rem(number, per)]

    def own_rows(turn, which, value):
        stage[turn, which, 0] = value[:, :HALF].astype(BF16)
        stage[turn, which, 1] = value[:, HALF:].astype(BF16)
        own = at_block(turn, which, block(which, False, 0))
        own[core] = stage[turn, which, core]

    def gather_start(turn, which):
        own = at_block(turn, which, block(which, False, 0)).at[core]
        for other, step in far_steps + near_steps:
            if abs(step) == 2:
                sem = g2_recv.at[turn, which, int(other), int(step < 0)]
            else:
                sem = gb_recv.at[turn, which]
            for to_core in range(2):
                send(stage.at[turn, which, to_core], own, gb_send.at[turn, which], sem,
                     device(which, other, step, to_core))
        send(stage.at[turn, which, 1 - core], own,
             gm_send.at[turn, which], gm_recv.at[turn, which], mate)

    def gather_relay(turn, which, other):
        for way, step in ((0, 1), (1, -1)):
            here = at_block(turn, which, block(which, other, -2 * step))
            awaits(here, g2_recv.at[turn, which, int(other), way])
            part = here.at[way]
            send(part, part, gb_send.at[turn, which], gb_recv.at[turn, which], along(which, 2 * step))
            send(here, here, gb_send.at[turn, which], gb_recv.at[turn, which], along(which, step))

    def gather_end(turn, which):
        awaits(sums.at[turn, which, pl.ds(0, 11)], gb_recv.at[turn, which])
        own = at_block(turn, which, block(which, False, 0))
        awaits(own.at[1 - core], gm_recv.at[turn, which])

    def marks(cell, slot):
        return meta[cell, pl.ds(slot, 1), :]

    def spread_users(turn):
        panel = panels[turn][ITEMS]
        for cell in range(2):
            for slot in range(SLOTS):
                rows = panel[meta_smem[cell, slot, 0] & 7].reshape(TILE, HALF)
                prod[cell * SLOTS + slot] = jnp.dot(
                    tiles[cell, slot], rows, preferred_element_type=F32
                )

        def add(number, carry):
            start = pl.ds(pl.multiple_of(lax.rem(number, 4) * ROWS, ROWS), ROWS)
            for cell in range(2):
                total = jnp.zeros((ROWS, HALF), F32)
                for slot in range(SLOTS):
                    weight = jnp.where((marks(cell, slot) >> 3) == number // 4, 1.0, 0.0)
                    total += weight.astype(F32) * prod[cell * SLOTS + slot, start, :]
                sums[turn, USERS, number, cell] = total.astype(BF16)
            return carry

        lax.fori_loop(0, BLOCKS, add, 0)

    def spread_items(turn):
        panel = panels[turn][USERS]
        for cell in range(2):
            for slot in range(SLOTS):
                tile = (meta_smem[cell, slot, 0] >> 3) & 3
                rows = panel[tile, :, cell].reshape(TILE, HALF)
                prod[cell * SLOTS + slot] = jnp.dot(
                    tiles_t[cell, slot], rows, preferred_element_type=F32
                )

        def add(number, carry):
            for owner in range(2):
                start = (lax.rem(number, 2) * 2 + owner) * ROWS
                start = pl.ds(pl.multiple_of(start, ROWS), ROWS)
                total = jnp.zeros((ROWS, HALF), F32)
                for cell in range(2):
                    for slot in range(SLOTS):
                        weight = jnp.where((marks(cell, slot) & 71) == number // 2, 1.0, 0.0)
                        total += weight.astype(F32) * prod[cell * SLOTS + slot, start, :]
                sums[turn, ITEMS, number, owner] = total.astype(BF16)
            return carry

        lax.fori_loop(0, BLOCKS, add, 0)

    def scatter_start(turn, which):
        out = s_send.at[turn, which]
        for other in (True, False):
            e = int(other)
            for way, step in ((0, 1), (1, -1)):
                sem = sf_recv.at[turn, which, e, way]
                send(sums.at[turn, which, block(which, other, 4), way],
                     far.at[turn, which, e, way, 2], out, sem, along(which, 2 * step))
                send(sums.at[turn, which, block(which, other, 3 * step)],
                     far.at[turn, which, e, way, pl.ds(0, 2)], out, sem, along(which, step))
        for other, step in near_steps:
            part = 0 if step == 0 else 1 + int(step < 0)
            for to_core in range(2):
                send_last(turn, which, other, step, part, to_core,
                          sums.at[turn, which, block(which, other, step), to_core])
        send(sums.at[turn, which, block(which, False, 0), 1 - core],
             last.at[turn, which, core * 10], sm_send.at[turn, which], sl_recv.at[turn, which], mate)

    def send_last(turn, which, other, step, part, to_core, source):
        send(source, last.at[turn, which, core * 10 + int(other) * 5 + part],
             s_send.at[turn, which], sl_recv.at[turn, which], device(which, other, step, to_core))

    def scatter_relay(turn, which, other):
        e = int(other)
        for way, step in ((0, 1), (1, -1)):
            came = far.at[turn, which, e, way]
            awaits(came, sf_recv.at[turn, which, e, way])
            mine = sums.at[turn, which, block(which, other, 2 * step)]
            for owner in range(2):
                total = mine[owner].astype(F32) + came[owner].astype(F32)
                if owner == way:
                    total += came[2].astype(F32)
                relayed[turn, which, e, way, owner] = total.astype(BF16)
            for to_core in range(2):
                send_last(turn, which, other, 2 * step, 3 + way, to_core,
                          relayed.at[turn, which, e, way, to_core])

    def scatter_end(turn, which):
        awaits(last.at[turn, which, pl.ds(0, 19)], sl_recv.at[turn, which])
        last[turn, which, core * 10] = sums[turn, which, block(which, False, 0), core]
        sides = []
        for side in range(2):
            total = last[turn, which, side * 10].astype(F32)
            for part in range(1, 10):
                total += last[turn, which, side * 10 + part].astype(F32)
            sides.append(total)
        return jnp.concatenate(sides, axis=1)

    def prepare():
        user_base = (row * BLOCKS + col) * ROWS
        item_base = (col * 2 * BLOCKS + row) * ROWS
        places = lax.broadcasted_iota(jnp.int32, (ROWS, uid_ref.shape[1]), 0)
        hot = jnp.where(places == uid_ref[...] - user_base, 1.0, 0.0).astype(F32)
        user_hot[...] = hot.astype(BF16)
        user_hot_t[...] = jnp.concatenate([hot] * 3, axis=0).T.astype(BF16)
        hot = jnp.where(places == nid_ref[...] - item_base, 1.0, 0.0).astype(F32)
        hot = hot - jnp.where(places == pid_ref[...] - item_base, 1.0, 0.0).astype(F32)
        item_hot[...] = hot.astype(BF16)
        item_hot_t[...] = jnp.concatenate([hot] * 3, axis=0).T.astype(BF16)

    both = (ITEMS, USERS)

    def propagate(turn):
        for which in both:
            gather_start(turn, which)
        if turn == 0:
            send(tiles_hbm, tiles.at[core], tile_send, tile_recv, mate)
            send(meta.at[core], meta.at[core], meta_send, meta_recv, mate)
            for copy in ids_load:
                copy.wait()
            prepare()
        for which in both:
            gather_relay(turn, which, False)
        for which in both:
            gather_relay(turn, which, True)
        if turn == 0:
            tiles_load.wait()
            awaits(meta.at[1 - core], meta_recv)
            fill = pltpu.make_async_copy(meta, meta_smem, meta_sem)
            fill.start()
            fill.wait()
            awaits(tiles.at[1 - core], tile_recv)
            for cell in range(2):
                for slot in range(SLOTS):
                    tiles_t[cell, slot] = tiles[cell, slot].T
        gather_end(turn, ITEMS)
        spread_users(turn)
        scatter_start(turn, USERS)
        gather_end(turn, USERS)
        spread_items(turn)
        scatter_start(turn, ITEMS)
        for other in (True, False):
            for which in (USERS, ITEMS):
                scatter_relay(turn, which, other)
        return scatter_end(turn, USERS), scatter_end(turn, ITEMS)

    items_load.wait()
    own_rows(0, ITEMS, items_ref[...])
    users_load.wait()
    own_rows(0, USERS, users_ref[...])
    pl.semaphore_wait(barrier, len(peers))
    first_users, first_items = propagate(0)
    final_users = 0.5 * (users_ref[...] + first_users)
    final_items = 0.5 * (items_ref[...] + first_items)

    dot = functools.partial(jnp.dot, preferred_element_type=F32)
    chosen = dot(user_hot_t[...], split(final_users, 3))
    against = dot(item_hot_t[...], split(final_items, 3))
    score = -jnp.sum(chosen * against, axis=1, keepdims=True)
    back = jax.nn.sigmoid(-score)
    hot = user_hot[...]
    grad_users = dot(jnp.concatenate([hot] * 3, axis=1), split(back * against, 3))
    hot = item_hot[...]
    grad_items = dot(jnp.concatenate([hot] * 3, axis=1), split(back * chosen, 3))

    own_rows(1, ITEMS, grad_items)
    own_rows(1, USERS, grad_users)
    back_users, back_items = propagate(1)
    out_users_ref[...] = 0.5 * grad_users + 0.5 * back_users
    out_items_ref[...] = 0.5 * grad_items + 0.5 * back_items

    sent(tiles_hbm, tile_send)
    sent(meta.at[core], meta_send)
    for turn in range(2):
        for which in (USERS, ITEMS):
            sent(stage.at[turn, which, core], gm_send.at[turn, which])
            sent(sums.at[turn, which, pl.ds(0, 15)], gb_send.at[turn, which])
            sent(sums.at[turn, which, pl.ds(0, 15)], s_send.at[turn, which])
            sent(stage.at[turn, which, core], sm_send.at[turn, which])


def on_device(users, items, tiles, tile_pos, tile_count, user_ids, pos_ids, neg_ids):
    vmem = pl.BlockSpec(memory_space=pltpu.VMEM)
    dma = pltpu.SemaphoreType.DMA
    batch = user_ids.shape[0]
    cut = (2, ROWS, HALF)
    return pl.pallas_call(
        kernel,
        out_shape=(
            jax.ShapeDtypeStruct((ROWS, WIDTH), F32),
            jax.ShapeDtypeStruct((ROWS, WIDTH), F32),
        ),
        in_specs=[pl.BlockSpec(memory_space=pl.ANY)] * 8,
        out_specs=(vmem, vmem),
        scratch_shapes=[
            pltpu.VMEM((ROWS, WIDTH), F32),
            pltpu.VMEM((ROWS, WIDTH), F32),
            pltpu.SMEM((1, SLOTS), jnp.int32),
            pltpu.SMEM((1, 1), jnp.int32),
            pltpu.VMEM((1, batch), jnp.int32),
            pltpu.VMEM((1, batch), jnp.int32),
            pltpu.VMEM((1, batch), jnp.int32),
            pltpu.VMEM((2, SLOTS, TILE, TILE), BF16),
            pltpu.VMEM((2, SLOTS, TILE, TILE), BF16),
            pltpu.VMEM((2, 8, HALF), jnp.int32),
            pltpu.SMEM((2, 8, HALF), jnp.int32),
            pltpu.VMEM((ROWS, batch), BF16),
            pltpu.VMEM((ROWS, batch), BF16),
            pltpu.VMEM((batch, 3 * ROWS), BF16),
            pltpu.VMEM((batch, 3 * ROWS), BF16),
            pltpu.VMEM((4, 4) + cut, BF16),
            pltpu.VMEM((4, 4) + cut, BF16),
            pltpu.VMEM((8, 2) + cut, BF16),
            pltpu.VMEM((8, 2) + cut, BF16),
            pltpu.VMEM((2, 2) + cut, BF16),
            pltpu.VMEM((2 * SLOTS, TILE, HALF), F32),
            pltpu.VMEM((2, 2, BLOCKS) + cut, BF16),
            pltpu.VMEM((2, 2, 2, 2, 3, ROWS, HALF), BF16),
            pltpu.VMEM((2, 2, 2, 2) + cut, BF16),
            pltpu.VMEM((2, 2, 20, ROWS, HALF), BF16),
            dma((8,)),
            dma,
            dma,
            dma,
            dma,
            dma,
            dma((2, 2)),
            dma((2, 2)),
            dma((2, 2, 2, 2)),
            dma((2, 2)),
            dma((2, 2)),
            dma((2, 2, 2, 2)),
            dma((2, 2)),
            dma((2, 2)),
            dma((2, 2)),
        ],
        compiler_params=pltpu.CompilerParams(
            collective_id=0, has_side_effects=True, vmem_limit_bytes=60 << 20
        ),
        name="propagation_layer",
    )(
        users,
        items,
        tile_pos.reshape(1, SLOTS),
        tile_count,
        user_ids.reshape(1, batch),
        pos_ids.reshape(1, batch),
        neg_ids.reshape(1, batch),
        tiles.reshape(SLOTS, TILE, TILE),
    )


def solution(mesh):
    placed = (
        P(("row", "col"), None),
        P(("col", "row"), None),
        P("row", "col", None, None, None),
        P("row", "col", None),
        P("row", "col"),
        P(("row", "col")),
        P(("row", "col")),
        P(("row", "col")),
    )
    return jax.shard_map(
        on_device,
        mesh=mesh,
        in_specs=placed,
        out_specs=(P(("row", "col"), None), P(("col", "row"), None)),
        check_vma=False,
    )
```

```python
import functools

import jax
import jax.numpy as jnp
from jax import lax
from jax.experimental import pallas as pl
from jax.experimental.pallas import tpu as pltpu
from jax.sharding import PartitionSpec as P

MESH = pl.DeviceIdType.MESH
BF16 = jnp.bfloat16
F32 = jnp.float32
SLOTS = 4
ROWS = 64
HALF = 128
WIDTH = 256
TILE = 256
RING = 8
BLOCKS = 16
USERS, ITEMS = 0, 1


def split(value, parts):
    terms = []
    for part in range(parts):
        term = value.astype(BF16)
        terms.append(term)
        value = value - term.astype(F32)
    return jnp.concatenate(terms, axis=0)


def kernel(
    users_hbm,
    items_hbm,
    pos_hbm,
    count_hbm,
    uid_hbm,
    pid_hbm,
    nid_hbm,
    tiles_hbm,
    out_ref,
    users_ref,
    items_ref,
    pos_ref,
    count_ref,
    uid_ref,
    pid_ref,
    nid_ref,
    tiles,
    tiles_t,
    meta,
    meta_smem,
    user_hot,
    item_hot,
    user_hot_t,
    item_hot_t,
    user_panel_0,
    user_panel_1,
    item_panel_0,
    item_panel_1,
    stage,
    prod,
    exact,
    sums,
    far,
    cross,
    paired,
    relayed,
    last,
    load_sem,
    tile_send,
    tile_recv,
    meta_sem,
    meta_send,
    meta_recv,
    gm_send,
    gm_recv,
    g1_recv,
    g2_recv,
    gb_send,
    gb_recv,
    sf_recv,
    sx_recv,
    sl_recv,
    s_send,
    sm_send,
):
    row = lax.axis_index("row")
    col = lax.axis_index("col")
    core = lax.rem(row, 2)
    group = row // 2
    mate = (row + 1 - 2 * core, col)
    x_at = (col // RING, group // RING)
    ring_at = (lax.rem(col, RING), lax.rem(group, RING))

    def block(which, other, step):
        x = 1 - x_at[which] if other else x_at[which]
        return x * RING + lax.rem(ring_at[which] + step + RING, RING)

    def device(which, other, step, to_core):
        number = block(which, other, step)
        if which == USERS:
            return (group * 2 + to_core, number)
        return (number * 2 + to_core, col)

    def along(which, step):
        return device(which, False, step, core)

    def send(source, target, send_sem, recv_sem, to):
        pltpu.make_async_remote_copy(
            src_ref=source, dst_ref=target, send_sem=send_sem, recv_sem=recv_sem,
            device_id=to, device_id_type=MESH,
        ).start()

    def awaits(ref, sem):
        pltpu.make_async_remote_copy(
            src_ref=ref, dst_ref=ref, send_sem=sem, recv_sem=sem,
            device_id=mate, device_id_type=MESH,
        ).wait_recv()

    def sent(ref, sem):
        pltpu.make_async_remote_copy(
            src_ref=ref, dst_ref=ref, send_sem=sem, recv_sem=sem,
            device_id=mate, device_id_type=MESH,
        ).wait_send()

    def load(number, source, target):
        copy = pltpu.make_async_copy(source, target, load_sem.at[number])
        copy.start()
        return copy

    items_load = load(0, items_hbm, items_ref)
    users_load = load(1, users_hbm, users_ref)
    pos_load = load(2, pos_hbm, pos_ref)
    count_load = load(3, count_hbm, count_ref)
    ids_load = [
        load(4, uid_hbm, uid_ref), load(5, pid_hbm, pid_ref), load(6, nid_hbm, nid_ref)
    ]
    tiles_load = load(7, tiles_hbm, tiles.at[core])

    barrier = pltpu.get_barrier_semaphore()
    far_steps = [(other, step) for step in (2, -2) for other in (True, False)]
    near_steps = [(False, 1), (False, -1), (True, 0)]
    peers = [mate]
    for which in (USERS, ITEMS):
        for other, step in far_steps + near_steps:
            peers += [device(which, other, step, to_core) for to_core in range(2)]
    for peer in peers:
        pl.semaphore_signal(barrier, 1, device_id=peer, device_id_type=MESH)

    pos_load.wait()
    count_load.wait()
    filled = jnp.full((8, HALF), count_ref[0, 0], jnp.int32)
    slot_of = lax.broadcasted_iota(jnp.int32, (8, HALF), 0)
    placed = jnp.full((8, HALF), pos_ref[0, 0], jnp.int32)
    for slot in range(1, SLOTS):
        placed = jnp.where(slot_of == slot, jnp.full((8, HALF), pos_ref[0, slot], jnp.int32), placed)
    meta[core] = jnp.where(slot_of < filled, placed, placed + 64)

    panels = ((user_panel_0, item_panel_0), (user_panel_1, item_panel_1))

    def at_block(turn, which, number):
        per = 4 if which == USERS else 2
        return panels[turn][which].at[number // per, lax.rem(number, per)]

    def own_rows(turn, which, value):
        stage[turn, which, 0] = value[:, :HALF].astype(BF16)
        stage[turn, which, 1] = value[:, HALF:].astype(BF16)
        own = at_block(turn, which, block(which, False, 0))
        own[core] = stage[turn, which, core]

    def gather_start(turn, which):
        own = at_block(turn, which, block(which, False, 0)).at[core]
        for other, step in far_steps + near_steps:
            if abs(step) == 2:
                sem = g2_recv.at[turn, which, int(other), int(step < 0)]
            elif abs(step) == 1:
                sem = g1_recv.at[turn, which, int(step < 0)]
            else:
                sem = gb_recv.at[turn, which]
            for to_core in range(2):
                send(stage.at[turn, which, to_core], own, gb_send.at[turn, which], sem,
                     device(which, other, step, to_core))
        send(stage.at[turn, which, 1 - core], own,
             gm_send.at[turn, which], gm_recv.at[turn, which], mate)

    def gather_relay(turn, which, other):
        for way, step in ((0, 1), (1, -1)):
            here = at_block(turn, which, block(which, other, -2 * step))
            awaits(here, g2_recv.at[turn, which, int(other), way])
            part = here.at[way]
            send(part, part, gb_send.at[turn, which], gb_recv.at[turn, which], along(which, 2 * step))
            send(here, here, gb_send.at[turn, which], gb_recv.at[turn, which], along(which, step))

    def gather_cross(turn, which):
        for way, step in ((0, 1), (1, -1)):
            here = at_block(turn, which, block(which, False, -step))
            awaits(here, g1_recv.at[turn, which, way])
            send(here, here, gb_send.at[turn, which], gb_recv.at[turn, which],
                 device(which, True, 0, core))

    def gather_end(turn, which):
        awaits(sums.at[turn, which, pl.ds(0, 9)], gb_recv.at[turn, which])
        own = at_block(turn, which, block(which, False, 0))
        awaits(own.at[1 - core], gm_recv.at[turn, which])

    def marks(cell, slot):
        return meta[cell, pl.ds(slot, 1), :]

    def spread_users(turn):
        panel = panels[turn][ITEMS]
        for cell in range(2):
            for slot in range(SLOTS):
                rows = panel[meta_smem[cell, slot, 0] & 7].reshape(TILE, HALF)
                prod[cell * SLOTS + slot] = jnp.dot(
                    tiles[cell, slot], rows, preferred_element_type=F32
                )

        def add(number, carry):
            start = pl.ds(pl.multiple_of(lax.rem(number, 4) * ROWS, ROWS), ROWS)
            for cell in range(2):
                total = jnp.zeros((ROWS, HALF), F32)
                for slot in range(SLOTS):
                    weight = jnp.where((marks(cell, slot) >> 3) == number // 4, 1.0, 0.0)
                    total += weight.astype(F32) * prod[cell * SLOTS + slot, start, :]
                exact[USERS, number, cell] = total
                sums[turn, USERS, number, cell] = total.astype(BF16)
            return carry

        lax.fori_loop(0, BLOCKS, add, 0)

    def spread_items(turn):
        panel = panels[turn][USERS]
        for cell in range(2):
            for slot in range(SLOTS):
                tile = (meta_smem[cell, slot, 0] >> 3) & 3
                rows = panel[tile, :, cell].reshape(TILE, HALF)
                prod[cell * SLOTS + slot] = jnp.dot(
                    tiles_t[cell, slot], rows, preferred_element_type=F32
                )

        def add(number, carry):
            for owner in range(2):
                start = (lax.rem(number, 2) * 2 + owner) * ROWS
                start = pl.ds(pl.multiple_of(start, ROWS), ROWS)
                total = jnp.zeros((ROWS, HALF), F32)
                for cell in range(2):
                    for slot in range(SLOTS):
                        weight = jnp.where((marks(cell, slot) & 71) == number // 2, 1.0, 0.0)
                        total += weight.astype(F32) * prod[cell * SLOTS + slot, start, :]
                exact[ITEMS, number, owner] = total
                sums[turn, ITEMS, number, owner] = total.astype(BF16)
            return carry

        lax.fori_loop(0, BLOCKS, add, 0)

    def scatter_start(turn, which):
        out = s_send.at[turn, which]
        for other in (True, False):
            e = int(other)
            for way, step in ((0, 1), (1, -1)):
                sem = sf_recv.at[turn, which, e, way]
                send(sums.at[turn, which, block(which, other, 4), way],
                     far.at[turn, which, e, way, 2], out, sem, along(which, 2 * step))
                send(sums.at[turn, which, block(which, other, 3 * step)],
                     far.at[turn, which, e, way, pl.ds(0, 2)], out, sem, along(which, step))
        for way, step in ((0, 1), (1, -1)):
            send(sums.at[turn, which, block(which, True, step)], cross.at[turn, which, way],
                 out, sx_recv.at[turn, which], device(which, True, 0, core))
        for to_core in range(2):
            send_last(turn, which, True, 0, 5, to_core,
                      sums.at[turn, which, block(which, True, 0), to_core])
        send(sums.at[turn, which, block(which, False, 0), 1 - core],
             last.at[turn, which, core * 8], sm_send.at[turn, which], sl_recv.at[turn, which], mate)

    def send_last(turn, which, other, step, part, to_core, source):
        send(source, last.at[turn, which, core * 8 + part],
             s_send.at[turn, which], sl_recv.at[turn, which], device(which, other, step, to_core))

    def scatter_near(turn, which):
        awaits(cross.at[turn, which], sx_recv.at[turn, which])
        for way, step in ((0, 1), (1, -1)):
            number = block(which, False, step)
            for to_core in range(2):
                total = exact[which, number, to_core] + cross[turn, which, way, to_core].astype(F32)
                paired[turn, which, way, to_core] = total.astype(BF16)
            for to_core in range(2):
                send_last(turn, which, False, step, 1 + way, to_core,
                          paired.at[turn, which, way, to_core])

    def scatter_relay(turn, which, other):
        e = int(other)
        for way, step in ((0, 1), (1, -1)):
            came = far.at[turn, which, e, way]
            awaits(came, sf_recv.at[turn, which, e, way])
            mine = exact.at[which, block(which, other, 2 * step)]
            for owner in range(2):
                total = mine[owner] + came[owner].astype(F32)
                if owner == way:
                    total += came[2].astype(F32)
                relayed[turn, which, e, way, owner] = total.astype(BF16)
            for to_core in range(2):
                send_last(turn, which, other, 2 * step, (6 if other else 3) + way, to_core,
                          relayed.at[turn, which, e, way, to_core])

    def scatter_end(turn, which):
        awaits(last.at[turn, which, pl.ds(0, 15)], sl_recv.at[turn, which])
        last[turn, which, core * 8] = jnp.zeros((ROWS, HALF), BF16)
        own = exact[which, block(which, False, 0), core]
        sides = []
        for side in range(2):
            total = jnp.where(core == side, own, 0.0)
            for part in range(8):
                total += last[turn, which, side * 8 + part].astype(F32)
            sides.append(total)
        return jnp.concatenate(sides, axis=1)

    def prepare():
        user_base = (row * BLOCKS + col) * ROWS
        item_base = (col * 2 * BLOCKS + row) * ROWS
        places = lax.broadcasted_iota(jnp.int32, (ROWS, uid_ref.shape[1]), 0)
        hot = jnp.where(places == uid_ref[...] - user_base, 1.0, 0.0).astype(F32)
        user_hot[...] = hot.astype(BF16)
        user_hot_t[...] = jnp.concatenate([hot] * 3, axis=0).T.astype(BF16)
        hot = jnp.where(places == nid_ref[...] - item_base, 1.0, 0.0).astype(F32)
        hot = hot - jnp.where(places == pid_ref[...] - item_base, 1.0, 0.0).astype(F32)
        item_hot[...] = hot.astype(BF16)
        item_hot_t[...] = jnp.concatenate([hot] * 3, axis=0).T.astype(BF16)

    both = (ITEMS, USERS)

    def propagate(turn):
        if turn == 0:
            send(tiles_hbm, tiles.at[core], tile_send, tile_recv, mate)
            send(meta.at[core], meta.at[core], meta_send, meta_recv, mate)
            for copy in ids_load:
                copy.wait()
            prepare()
        for which in both:
            gather_relay(turn, which, False)
        for which in both:
            gather_cross(turn, which)
        for which in both:
            gather_relay(turn, which, True)
        if turn == 0:
            tiles_load.wait()
            awaits(meta.at[1 - core], meta_recv)
            fill = pltpu.make_async_copy(meta, meta_smem, meta_sem)
            fill.start()
            fill.wait()
            awaits(tiles.at[1 - core], tile_recv)
            for cell in range(2):
                for slot in range(SLOTS):
                    tiles_t[cell, slot] = tiles[cell, slot].T
        gather_end(turn, ITEMS)
        spread_users(turn)
        scatter_start(turn, USERS)
        gather_end(turn, USERS)
        spread_items(turn)
        scatter_start(turn, ITEMS)
        for other in (True, False):
            for which in (USERS, ITEMS):
                scatter_relay(turn, which, other)
        for which in (USERS, ITEMS):
            scatter_near(turn, which)
        return scatter_end(turn, USERS), scatter_end(turn, ITEMS)

    items_load.wait()
    own_rows(0, ITEMS, items_ref[...])
    users_load.wait()
    own_rows(0, USERS, users_ref[...])
    pl.semaphore_wait(barrier, len(peers))
    for which in both:
        gather_start(0, which)
    first_users, first_items = propagate(0)
    final_users = 0.5 * (users_ref[...] + first_users)
    final_items = 0.5 * (items_ref[...] + first_items)

    dot = functools.partial(jnp.dot, preferred_element_type=F32)
    chosen = dot(user_hot_t[...], split(final_users, 3))
    against = dot(item_hot_t[...], split(final_items, 3))
    score = -jnp.sum(chosen * against, axis=1, keepdims=True)
    back = jax.nn.sigmoid(-score)
    hot = user_hot[...]
    grad_users = dot(jnp.concatenate([hot] * 2, axis=1), split(back * against, 2))
    own_rows(1, USERS, grad_users)
    gather_start(1, USERS)
    hot = item_hot[...]
    grad_items = dot(jnp.concatenate([hot] * 2, axis=1), split(back * chosen, 2))
    own_rows(1, ITEMS, grad_items)
    gather_start(1, ITEMS)
    back_users, back_items = propagate(1)
    out_ref[0] = 0.5 * grad_users + 0.5 * back_users
    out_ref[1] = 0.5 * grad_items + 0.5 * back_items

    sent(tiles_hbm, tile_send)
    sent(meta.at[core], meta_send)
    for turn in range(2):
        for which in (USERS, ITEMS):
            sent(stage.at[turn, which, core], gm_send.at[turn, which])
            sent(sums.at[turn, which, pl.ds(0, 15)], gb_send.at[turn, which])
            sent(sums.at[turn, which, pl.ds(0, 15)], s_send.at[turn, which])
            sent(stage.at[turn, which, core], sm_send.at[turn, which])


def on_device(users, items, tiles, tile_pos, tile_count, user_ids, pos_ids, neg_ids):
    vmem = pl.BlockSpec(memory_space=pltpu.VMEM)
    dma = pltpu.SemaphoreType.DMA
    batch = user_ids.shape[0]
    cut = (2, ROWS, HALF)
    out = pl.pallas_call(
        kernel,
        out_shape=jax.ShapeDtypeStruct((2, ROWS, WIDTH), F32),
        in_specs=[pl.BlockSpec(memory_space=pl.ANY)] * 8,
        out_specs=vmem,
        scratch_shapes=[
            pltpu.VMEM((ROWS, WIDTH), F32),
            pltpu.VMEM((ROWS, WIDTH), F32),
            pltpu.SMEM((1, SLOTS), jnp.int32),
            pltpu.SMEM((1, 1), jnp.int32),
            pltpu.VMEM((1, batch), jnp.int32),
            pltpu.VMEM((1, batch), jnp.int32),
            pltpu.VMEM((1, batch), jnp.int32),
            pltpu.VMEM((2, SLOTS, TILE, TILE), BF16),
            pltpu.VMEM((2, SLOTS, TILE, TILE), BF16),
            pltpu.VMEM((2, 8, HALF), jnp.int32),
            pltpu.SMEM((2, 8, HALF), jnp.int32),
            pltpu.VMEM((ROWS, batch), BF16),
            pltpu.VMEM((ROWS, batch), BF16),
            pltpu.VMEM((batch, 3 * ROWS), BF16),
            pltpu.VMEM((batch, 3 * ROWS), BF16),
            pltpu.VMEM((4, 4) + cut, BF16),
            pltpu.VMEM((4, 4) + cut, BF16),
            pltpu.VMEM((8, 2) + cut, BF16),
            pltpu.VMEM((8, 2) + cut, BF16),
            pltpu.VMEM((2, 2) + cut, BF16),
            pltpu.VMEM((2 * SLOTS, TILE, HALF), F32),
            pltpu.VMEM((2, BLOCKS) + cut, F32),
            pltpu.VMEM((2, 2, BLOCKS) + cut, BF16),
            pltpu.VMEM((2, 2, 2, 2, 3, ROWS, HALF), BF16),
            pltpu.VMEM((2, 2, 2) + cut, BF16),
            pltpu.VMEM((2, 2, 2) + cut, BF16),
            pltpu.VMEM((2, 2, 2, 2) + cut, BF16),
            pltpu.VMEM((2, 2, 16, ROWS, HALF), BF16),
            dma((8,)),
            dma,
            dma,
            dma,
            dma,
            dma,
            dma((2, 2)),
            dma((2, 2)),
            dma((2, 2, 2)),
            dma((2, 2, 2, 2)),
            dma((2, 2)),
            dma((2, 2)),
            dma((2, 2, 2, 2)),
            dma((2, 2)),
            dma((2, 2)),
            dma((2, 2)),
            dma((2, 2)),
        ],
        compiler_params=pltpu.CompilerParams(
            collective_id=0, has_side_effects=True, vmem_limit_bytes=60 << 20
        ),
        name="propagation_layer",
    )(
        users,
        items,
        tile_pos.reshape(1, SLOTS),
        tile_count,
        user_ids.reshape(1, batch),
        pos_ids.reshape(1, batch),
        neg_ids.reshape(1, batch),
        tiles.reshape(SLOTS, TILE, TILE),
    )
    return out[0], out[1]


def solution(mesh):
    placed = (
        P(("row", "col"), None),
        P(("col", "row"), None),
        P("row", "col", None, None, None),
        P("row", "col", None),
        P("row", "col"),
        P(("row", "col")),
        P(("row", "col")),
        P(("row", "col")),
    )
    return jax.shard_map(
        on_device,
        mesh=mesh,
        in_specs=placed,
        out_specs=(P(("row", "col"), None), P(("col", "row"), None)),
        check_vma=False,
    )
```

```python
import functools

import jax
import jax.numpy as jnp
from jax import lax
from jax.experimental import pallas as pl
from jax.experimental.pallas import tpu as pltpu
from jax.sharding import PartitionSpec as P

MESH = pl.DeviceIdType.MESH
BF16 = jnp.bfloat16
F32 = jnp.float32
SLOTS = 4
ROWS = 64
HALF = 128
WIDTH = 256
TILE = 256
RING = 8
BLOCKS = 16
USERS, ITEMS = 0, 1


def split(value, parts):
    terms = []
    for part in range(parts):
        term = value.astype(BF16)
        terms.append(term)
        value = value - term.astype(F32)
    return jnp.concatenate(terms, axis=0)


def kernel(
    users_hbm,
    items_hbm,
    pos_hbm,
    count_hbm,
    uid_hbm,
    pid_hbm,
    nid_hbm,
    tiles_hbm,
    out_ref,
    users_ref,
    items_ref,
    pos_ref,
    count_ref,
    uid_ref,
    pid_ref,
    nid_ref,
    tiles,
    tiles_t,
    meta,
    meta_smem,
    user_hot,
    item_hot,
    user_hot_t,
    item_hot_t,
    user_panel_0,
    user_panel_1,
    item_panel_0,
    item_panel_1,
    stage,
    prod,
    exact,
    sums,
    far,
    cross,
    paired,
    relayed,
    last,
    load_sem,
    tile_send,
    tile_recv,
    meta_sem,
    meta_send,
    meta_recv,
    gm_send,
    gm_recv,
    g1_recv,
    g2_recv,
    gb_send,
    gb_recv,
    sf_recv,
    sx_recv,
    sl_recv,
    s_send,
    sm_send,
):
    row = lax.axis_index("row")
    col = lax.axis_index("col")
    core = lax.rem(row, 2)
    group = row // 2
    mate = (row + 1 - 2 * core, col)
    x_at = (col // RING, group // RING)
    ring_at = (lax.rem(col, RING), lax.rem(group, RING))

    def block(which, other, step):
        x = 1 - x_at[which] if other else x_at[which]
        return x * RING + lax.rem(ring_at[which] + step + RING, RING)

    def device(which, other, step, to_core):
        number = block(which, other, step)
        if which == USERS:
            return (group * 2 + to_core, number)
        return (number * 2 + to_core, col)

    def along(which, step):
        return device(which, False, step, core)

    def send(source, target, send_sem, recv_sem, to):
        pltpu.make_async_remote_copy(
            src_ref=source, dst_ref=target, send_sem=send_sem, recv_sem=recv_sem,
            device_id=to, device_id_type=MESH,
        ).start()

    def awaits(ref, sem):
        pltpu.make_async_remote_copy(
            src_ref=ref, dst_ref=ref, send_sem=sem, recv_sem=sem,
            device_id=mate, device_id_type=MESH,
        ).wait_recv()

    def sent(ref, sem):
        pltpu.make_async_remote_copy(
            src_ref=ref, dst_ref=ref, send_sem=sem, recv_sem=sem,
            device_id=mate, device_id_type=MESH,
        ).wait_send()

    def load(number, source, target):
        copy = pltpu.make_async_copy(source, target, load_sem.at[number])
        copy.start()
        return copy

    items_load = load(0, items_hbm, items_ref)
    users_load = load(1, users_hbm, users_ref)
    pos_load = load(2, pos_hbm, pos_ref)
    count_load = load(3, count_hbm, count_ref)
    ids_load = [
        load(4, uid_hbm, uid_ref), load(5, pid_hbm, pid_ref), load(6, nid_hbm, nid_ref)
    ]
    tiles_load = load(7, tiles_hbm, tiles.at[core])

    barrier = pltpu.get_barrier_semaphore()
    far_steps = [(other, step) for step in (2, -2) for other in (True, False)]
    near_steps = [(False, 1), (False, -1), (True, 0)]
    peers = [mate]
    for which in (USERS, ITEMS):
        for other, step in far_steps + near_steps:
            peers += [device(which, other, step, to_core) for to_core in range(2)]
    for peer in peers:
        pl.semaphore_signal(barrier, 1, device_id=peer, device_id_type=MESH)

    pos_load.wait()
    count_load.wait()
    filled = jnp.full((8, HALF), count_ref[0, 0], jnp.int32)
    slot_of = lax.broadcasted_iota(jnp.int32, (8, HALF), 0)
    placed = jnp.full((8, HALF), pos_ref[0, 0], jnp.int32)
    for slot in range(1, SLOTS):
        placed = jnp.where(slot_of == slot, jnp.full((8, HALF), pos_ref[0, slot], jnp.int32), placed)
    meta[core] = jnp.where(slot_of < filled, placed, placed + 64)

    panels = ((user_panel_0, item_panel_0), (user_panel_1, item_panel_1))

    def at_block(turn, which, number):
        per = 4 if which == USERS else 2
        return panels[turn][which].at[number // per, lax.rem(number, per)]

    def own_rows(turn, which, value):
        stage[turn, which, 0] = value[:, :HALF].astype(BF16)
        stage[turn, which, 1] = value[:, HALF:].astype(BF16)
        own = at_block(turn, which, block(which, False, 0))
        own[core] = stage[turn, which, core]

    def gather_start(turn, which):
        own = at_block(turn, which, block(which, False, 0)).at[core]
        for other, step in far_steps + near_steps:
            if abs(step) == 2:
                sem = g2_recv.at[turn, which, int(other), int(step < 0)]
            elif abs(step) == 1:
                sem = g1_recv.at[turn, which, int(step < 0)]
            else:
                sem = gb_recv.at[turn, which]
            for to_core in range(2):
                send(stage.at[turn, which, to_core], own, gb_send.at[turn, which], sem,
                     device(which, other, step, to_core))
        send(stage.at[turn, which, 1 - core], own,
             gm_send.at[turn, which], gm_recv.at[turn, which], mate)

    def gather_relay(turn, which, other):
        for way, step in ((0, 1), (1, -1)):
            here = at_block(turn, which, block(which, other, -2 * step))
            awaits(here, g2_recv.at[turn, which, int(other), way])
            part = here.at[way]
            send(part, part, gb_send.at[turn, which], gb_recv.at[turn, which], along(which, 2 * step))
            send(here, here, gb_send.at[turn, which], gb_recv.at[turn, which], along(which, step))

    def gather_cross(turn, which):
        for way, step in ((0, 1), (1, -1)):
            here = at_block(turn, which, block(which, False, -step))
            awaits(here, g1_recv.at[turn, which, way])
            send(here, here, gb_send.at[turn, which], gb_recv.at[turn, which],
                 device(which, True, 0, core))

    def gather_end(turn, which):
        awaits(sums.at[turn, which, pl.ds(0, 9)], gb_recv.at[turn, which])
        own = at_block(turn, which, block(which, False, 0))
        awaits(own.at[1 - core], gm_recv.at[turn, which])

    def marks(cell, slot):
        return meta[cell, pl.ds(slot, 1), :]

    def spread_users(turn):
        panel = panels[turn][ITEMS]
        for cell in range(2):
            for slot in range(SLOTS):
                rows = panel[meta_smem[cell, slot, 0] & 7].reshape(TILE, HALF)
                prod[cell * SLOTS + slot] = jnp.dot(
                    tiles[cell, slot], rows, preferred_element_type=F32
                )

        def add(number, carry):
            start = pl.ds(pl.multiple_of(lax.rem(number, 4) * ROWS, ROWS), ROWS)
            for cell in range(2):
                total = jnp.zeros((ROWS, HALF), F32)
                for slot in range(SLOTS):
                    weight = jnp.where((marks(cell, slot) >> 3) == number // 4, 1.0, 0.0)
                    total += weight.astype(F32) * prod[cell * SLOTS + slot, start, :]
                exact[USERS, number, cell] = total
                sums[turn, USERS, number, cell] = total.astype(BF16)
            return carry

        lax.fori_loop(0, BLOCKS, add, 0, unroll=4)

    def spread_items(turn):
        panel = panels[turn][USERS]
        for cell in range(2):
            for slot in range(SLOTS):
                tile = (meta_smem[cell, slot, 0] >> 3) & 3
                rows = panel[tile, :, cell].reshape(TILE, HALF)
                prod[cell * SLOTS + slot] = jnp.dot(
                    tiles_t[cell, slot], rows, preferred_element_type=F32
                )

        def add(number, carry):
            for owner in range(2):
                start = (lax.rem(number, 2) * 2 + owner) * ROWS
                start = pl.ds(pl.multiple_of(start, ROWS), ROWS)
                total = jnp.zeros((ROWS, HALF), F32)
                for cell in range(2):
                    for slot in range(SLOTS):
                        weight = jnp.where((marks(cell, slot) & 71) == number // 2, 1.0, 0.0)
                        total += weight.astype(F32) * prod[cell * SLOTS + slot, start, :]
                exact[ITEMS, number, owner] = total
                sums[turn, ITEMS, number, owner] = total.astype(BF16)
            return carry

        lax.fori_loop(0, BLOCKS, add, 0, unroll=4)

    def scatter_start(turn, which):
        out = s_send.at[turn, which]
        for other in (True, False):
            e = int(other)
            for way, step in ((0, 1), (1, -1)):
                sem = sf_recv.at[turn, which, e, way]
                send(sums.at[turn, which, block(which, other, 4), way],
                     far.at[turn, which, e, way, 2], out, sem, along(which, 2 * step))
                send(sums.at[turn, which, block(which, other, 3 * step)],
                     far.at[turn, which, e, way, pl.ds(0, 2)], out, sem, along(which, step))
        for way, step in ((0, 1), (1, -1)):
            send(sums.at[turn, which, block(which, True, step)], cross.at[turn, which, way],
                 out, sx_recv.at[turn, which], device(which, True, 0, core))
        for to_core in range(2):
            send_last(turn, which, True, 0, 5, to_core,
                      sums.at[turn, which, block(which, True, 0), to_core])
        send(sums.at[turn, which, block(which, False, 0), 1 - core],
             last.at[turn, which, core * 8], sm_send.at[turn, which], sl_recv.at[turn, which], mate)

    def send_last(turn, which, other, step, part, to_core, source):
        send(source, last.at[turn, which, core * 8 + part],
             s_send.at[turn, which], sl_recv.at[turn, which], device(which, other, step, to_core))

    def scatter_near(turn, which):
        awaits(cross.at[turn, which], sx_recv.at[turn, which])
        for way, step in ((0, 1), (1, -1)):
            number = block(which, False, step)
            for to_core in range(2):
                total = exact[which, number, to_core] + cross[turn, which, way, to_core].astype(F32)
                paired[turn, which, way, to_core] = total.astype(BF16)
            for to_core in range(2):
                send_last(turn, which, False, step, 1 + way, to_core,
                          paired.at[turn, which, way, to_core])

    def scatter_relay(turn, which, other):
        e = int(other)
        for way, step in ((0, 1), (1, -1)):
            came = far.at[turn, which, e, way]
            awaits(came, sf_recv.at[turn, which, e, way])
            mine = exact.at[which, block(which, other, 2 * step)]
            for owner in range(2):
                total = mine[owner] + came[owner].astype(F32)
                if owner == way:
                    total += came[2].astype(F32)
                relayed[turn, which, e, way, owner] = total.astype(BF16)
            for to_core in range(2):
                send_last(turn, which, other, 2 * step, (6 if other else 3) + way, to_core,
                          relayed.at[turn, which, e, way, to_core])

    def scatter_end(turn, which):
        awaits(last.at[turn, which, pl.ds(0, 15)], sl_recv.at[turn, which])
        last[turn, which, core * 8] = jnp.zeros((ROWS, HALF), BF16)
        own = exact[which, block(which, False, 0), core]
        sides = []
        for side in range(2):
            total = jnp.where(core == side, own, 0.0)
            for part in range(8):
                total += last[turn, which, side * 8 + part].astype(F32)
            sides.append(total)
        return jnp.concatenate(sides, axis=1)

    def prepare():
        user_base = (row * BLOCKS + col) * ROWS
        item_base = (col * 2 * BLOCKS + row) * ROWS
        places = lax.broadcasted_iota(jnp.int32, (ROWS, uid_ref.shape[1]), 0)
        hot = jnp.where(places == uid_ref[...] - user_base, 1.0, 0.0).astype(F32)
        user_hot[...] = hot.astype(BF16)
        user_hot_t[...] = jnp.concatenate([hot] * 3, axis=0).T.astype(BF16)
        hot = jnp.where(places == nid_ref[...] - item_base, 1.0, 0.0).astype(F32)
        hot = hot - jnp.where(places == pid_ref[...] - item_base, 1.0, 0.0).astype(F32)
        item_hot[...] = hot.astype(BF16)
        item_hot_t[...] = jnp.concatenate([hot] * 3, axis=0).T.astype(BF16)

    both = (ITEMS, USERS)

    def propagate(turn):
        if turn == 0:
            send(tiles_hbm, tiles.at[core], tile_send, tile_recv, mate)
            send(meta.at[core], meta.at[core], meta_send, meta_recv, mate)
            for copy in ids_load:
                copy.wait()
            prepare()
        for which in both:
            gather_relay(turn, which, False)
        for which in both:
            gather_cross(turn, which)
        for which in both:
            gather_relay(turn, which, True)
        if turn == 0:
            tiles_load.wait()
            awaits(meta.at[1 - core], meta_recv)
            fill = pltpu.make_async_copy(meta, meta_smem, meta_sem)
            fill.start()
            fill.wait()
            awaits(tiles.at[1 - core], tile_recv)
            for cell in range(2):
                for slot in range(SLOTS):
                    tiles_t[cell, slot] = tiles[cell, slot].T
        gather_end(turn, ITEMS)
        spread_users(turn)
        scatter_start(turn, USERS)
        gather_end(turn, USERS)
        spread_items(turn)
        scatter_start(turn, ITEMS)
        for other in (True, False):
            for which in (USERS, ITEMS):
                scatter_relay(turn, which, other)
        for which in (USERS, ITEMS):
            scatter_near(turn, which)
        return scatter_end(turn, USERS), scatter_end(turn, ITEMS)

    items_load.wait()
    own_rows(0, ITEMS, items_ref[...])
    users_load.wait()
    own_rows(0, USERS, users_ref[...])
    pl.semaphore_wait(barrier, len(peers))
    for which in both:
        gather_start(0, which)
    first_users, first_items = propagate(0)
    final_users = 0.5 * (users_ref[...] + first_users)
    final_items = 0.5 * (items_ref[...] + first_items)

    dot = functools.partial(jnp.dot, preferred_element_type=F32)
    chosen = dot(user_hot_t[...], split(final_users, 3))
    against = dot(item_hot_t[...], split(final_items, 3))
    score = -jnp.sum(chosen * against, axis=1, keepdims=True)
    back = jax.nn.sigmoid(-score)
    hot = user_hot[...]
    grad_users = dot(jnp.concatenate([hot] * 2, axis=1), split(back * against, 2))
    own_rows(1, USERS, grad_users)
    gather_start(1, USERS)
    hot = item_hot[...]
    grad_items = dot(jnp.concatenate([hot] * 2, axis=1), split(back * chosen, 2))
    own_rows(1, ITEMS, grad_items)
    gather_start(1, ITEMS)
    back_users, back_items = propagate(1)
    out_ref[0] = 0.5 * grad_users + 0.5 * back_users
    out_ref[1] = 0.5 * grad_items + 0.5 * back_items

    sent(tiles_hbm, tile_send)
    sent(meta.at[core], meta_send)
    for turn in range(2):
        for which in (USERS, ITEMS):
            sent(stage.at[turn, which, core], gm_send.at[turn, which])
            sent(sums.at[turn, which, pl.ds(0, 15)], gb_send.at[turn, which])
            sent(sums.at[turn, which, pl.ds(0, 15)], s_send.at[turn, which])
            sent(stage.at[turn, which, core], sm_send.at[turn, which])


def in_hbm(value):
    return pltpu.with_memory_space_constraint(value, pltpu.HBM)


def on_device(users, items, tiles, tile_pos, tile_count, user_ids, pos_ids, neg_ids):
    vmem = pl.BlockSpec(memory_space=pltpu.VMEM)
    dma = pltpu.SemaphoreType.DMA
    batch = user_ids.shape[0]
    cut = (2, ROWS, HALF)
    out = pl.pallas_call(
        kernel,
        out_shape=jax.ShapeDtypeStruct((2, ROWS, WIDTH), F32),
        in_specs=[pl.BlockSpec(memory_space=pl.ANY)] * 8,
        out_specs=vmem,
        scratch_shapes=[
            pltpu.VMEM((ROWS, WIDTH), F32),
            pltpu.VMEM((ROWS, WIDTH), F32),
            pltpu.SMEM((1, SLOTS), jnp.int32),
            pltpu.SMEM((1, 1), jnp.int32),
            pltpu.VMEM((1, batch), jnp.int32),
            pltpu.VMEM((1, batch), jnp.int32),
            pltpu.VMEM((1, batch), jnp.int32),
            pltpu.VMEM((2, SLOTS, TILE, TILE), BF16),
            pltpu.VMEM((2, SLOTS, TILE, TILE), BF16),
            pltpu.VMEM((2, 8, HALF), jnp.int32),
            pltpu.SMEM((2, 8, HALF), jnp.int32),
            pltpu.VMEM((ROWS, batch), BF16),
            pltpu.VMEM((ROWS, batch), BF16),
            pltpu.VMEM((batch, 3 * ROWS), BF16),
            pltpu.VMEM((batch, 3 * ROWS), BF16),
            pltpu.VMEM((4, 4) + cut, BF16),
            pltpu.VMEM((4, 4) + cut, BF16),
            pltpu.VMEM((8, 2) + cut, BF16),
            pltpu.VMEM((8, 2) + cut, BF16),
            pltpu.VMEM((2, 2) + cut, BF16),
            pltpu.VMEM((2 * SLOTS, TILE, HALF), F32),
            pltpu.VMEM((2, BLOCKS) + cut, F32),
            pltpu.VMEM((2, 2, BLOCKS) + cut, BF16),
            pltpu.VMEM((2, 2, 2, 2, 3, ROWS, HALF), BF16),
            pltpu.VMEM((2, 2, 2) + cut, BF16),
            pltpu.VMEM((2, 2, 2) + cut, BF16),
            pltpu.VMEM((2, 2, 2, 2) + cut, BF16),
            pltpu.VMEM((2, 2, 16, ROWS, HALF), BF16),
            dma((8,)),
            dma,
            dma,
            dma,
            dma,
            dma,
            dma((2, 2)),
            dma((2, 2)),
            dma((2, 2, 2)),
            dma((2, 2, 2, 2)),
            dma((2, 2)),
            dma((2, 2)),
            dma((2, 2, 2, 2)),
            dma((2, 2)),
            dma((2, 2)),
            dma((2, 2)),
            dma((2, 2)),
        ],
        compiler_params=pltpu.CompilerParams(
            collective_id=0, has_side_effects=True, vmem_limit_bytes=40 << 20
        ),
        name="propagation_layer",
    )(
        in_hbm(users),
        in_hbm(items),
        in_hbm(tile_pos.reshape(1, SLOTS)),
        tile_count,
        in_hbm(user_ids.reshape(1, batch)),
        in_hbm(pos_ids.reshape(1, batch)),
        in_hbm(neg_ids.reshape(1, batch)),
        in_hbm(tiles.reshape(SLOTS, TILE, TILE)),
    )
    return out[0], out[1]


def solution(mesh):
    placed = (
        P(("row", "col"), None),
        P(("col", "row"), None),
        P("row", "col", None, None, None),
        P("row", "col", None),
        P("row", "col"),
        P(("row", "col")),
        P(("row", "col")),
        P(("row", "col")),
    )
    return jax.shard_map(
        on_device,
        mesh=mesh,
        in_specs=placed,
        out_specs=(P(("row", "col"), None), P(("col", "row"), None)),
        check_vma=False,
    )
```

```python
import functools

import jax
import jax.numpy as jnp
from jax import lax
from jax.experimental import pallas as pl
from jax.experimental.pallas import tpu as pltpu
from jax.sharding import PartitionSpec as P

MESH = pl.DeviceIdType.MESH
BF16 = jnp.bfloat16
F32 = jnp.float32
SLOTS = 4
ROWS = 64
HALF = 128
WIDTH = 256
TILE = 256
RING = 8
BLOCKS = 16
USERS, ITEMS = 0, 1


def split(value, parts):
    terms = []
    for part in range(parts):
        term = value.astype(BF16)
        terms.append(term)
        value = value - term.astype(F32)
    return jnp.concatenate(terms, axis=0)


def kernel(
    users_hbm,
    items_hbm,
    pos_hbm,
    count_hbm,
    uid_hbm,
    pid_hbm,
    nid_hbm,
    tiles_hbm,
    out_ref,
    users_ref,
    items_ref,
    pos_ref,
    count_ref,
    uid_ref,
    pid_ref,
    nid_ref,
    tiles,
    tiles_t,
    meta,
    meta_smem,
    user_hot,
    item_hot,
    user_hot_t,
    item_hot_t,
    user_panel_0,
    user_panel_1,
    item_panel_0,
    item_panel_1,
    stage,
    prod,
    exact,
    sums,
    far,
    cross,
    paired,
    relayed,
    last,
    load_sem,
    tile_send,
    tile_recv,
    meta_sem,
    meta_send,
    meta_recv,
    gm_send,
    gm_recv,
    g1_recv,
    g2_recv,
    gb_send,
    gb_recv,
    sf_recv,
    sx_recv,
    sl_recv,
    s_send,
    sm_send,
):
    row = lax.axis_index("row")
    col = lax.axis_index("col")
    core = lax.rem(row, 2)
    group = row // 2
    mate = (row + 1 - 2 * core, col)
    x_at = (col // RING, group // RING)
    ring_at = (lax.rem(col, RING), lax.rem(group, RING))

    def block(which, other, step):
        x = 1 - x_at[which] if other else x_at[which]
        return x * RING + lax.rem(ring_at[which] + step + RING, RING)

    def device(which, other, step, to_core):
        number = block(which, other, step)
        if which == USERS:
            return (group * 2 + to_core, number)
        return (number * 2 + to_core, col)

    def along(which, step):
        return device(which, False, step, core)

    def send(source, target, send_sem, recv_sem, to):
        pltpu.make_async_remote_copy(
            src_ref=source, dst_ref=target, send_sem=send_sem, recv_sem=recv_sem,
            device_id=to, device_id_type=MESH,
        ).start()

    def awaits(ref, sem):
        pltpu.make_async_remote_copy(
            src_ref=ref, dst_ref=ref, send_sem=sem, recv_sem=sem,
            device_id=mate, device_id_type=MESH,
        ).wait_recv()

    def sent(ref, sem):
        pltpu.make_async_remote_copy(
            src_ref=ref, dst_ref=ref, send_sem=sem, recv_sem=sem,
            device_id=mate, device_id_type=MESH,
        ).wait_send()

    def load(number, source, target):
        copy = pltpu.make_async_copy(source, target, load_sem.at[number])
        copy.start()
        return copy

    items_load = load(0, items_hbm, items_ref)
    users_load = load(1, users_hbm, users_ref)
    pos_load = load(2, pos_hbm, pos_ref)
    count_load = load(3, count_hbm, count_ref)
    ids_load = [
        load(4, uid_hbm, uid_ref), load(5, pid_hbm, pid_ref), load(6, nid_hbm, nid_ref)
    ]
    tiles_load = load(7, tiles_hbm, tiles.at[core])

    barrier = pltpu.get_barrier_semaphore()
    far_steps = [(other, step) for step in (2, -2) for other in (True, False)]
    near_steps = [(False, 1), (False, -1), (True, 0)]
    peers = [mate]
    for which in (USERS, ITEMS):
        for other, step in far_steps + near_steps:
            peers += [device(which, other, step, to_core) for to_core in range(2)]
    for peer in peers:
        pl.semaphore_signal(barrier, 1, device_id=peer, device_id_type=MESH)

    pos_load.wait()
    count_load.wait()
    filled = jnp.full((8, HALF), count_ref[0, 0], jnp.int32)
    slot_of = lax.broadcasted_iota(jnp.int32, (8, HALF), 0)
    placed = jnp.full((8, HALF), pos_ref[0, 0], jnp.int32)
    for slot in range(1, SLOTS):
        placed = jnp.where(slot_of == slot, jnp.full((8, HALF), pos_ref[0, slot], jnp.int32), placed)
    meta[core] = jnp.where(slot_of < filled, placed, placed + 64)

    panels = ((user_panel_0, item_panel_0), (user_panel_1, item_panel_1))

    def at_block(turn, which, number):
        per = 4 if which == USERS else 2
        return panels[turn][which].at[number // per, lax.rem(number, per)]

    def own_rows(turn, which, value):
        stage[turn, which, 0] = value[:, :HALF].astype(BF16)
        stage[turn, which, 1] = value[:, HALF:].astype(BF16)
        own = at_block(turn, which, block(which, False, 0))
        own[core] = stage[turn, which, core]

    def gather_start(turn, which):
        own = at_block(turn, which, block(which, False, 0)).at[core]
        for other, step in far_steps + near_steps:
            if abs(step) == 2:
                sem = g2_recv.at[turn, which, int(other), int(step < 0)]
            elif abs(step) == 1:
                sem = g1_recv.at[turn, which, int(step < 0)]
            else:
                sem = gb_recv.at[turn, which]
            for to_core in range(2):
                send(stage.at[turn, which, to_core], own, gb_send.at[turn, which], sem,
                     device(which, other, step, to_core))
        send(stage.at[turn, which, 1 - core], own,
             gm_send.at[turn, which], gm_recv.at[turn, which], mate)

    def gather_relay(turn, which, other):
        for way, step in ((0, 1), (1, -1)):
            here = at_block(turn, which, block(which, other, -2 * step))
            awaits(here, g2_recv.at[turn, which, int(other), way])
            part = here.at[way]
            send(part, part, gb_send.at[turn, which], gb_recv.at[turn, which], along(which, 2 * step))
            send(here, here, gb_send.at[turn, which], gb_recv.at[turn, which], along(which, step))

    def gather_cross(turn, which):
        for way, step in ((0, 1), (1, -1)):
            here = at_block(turn, which, block(which, False, -step))
            awaits(here, g1_recv.at[turn, which, way])
            send(here, here, gb_send.at[turn, which], gb_recv.at[turn, which],
                 device(which, True, 0, core))

    def gather_end(turn, which):
        awaits(sums.at[turn, which, pl.ds(0, 9)], gb_recv.at[turn, which])
        own = at_block(turn, which, block(which, False, 0))
        awaits(own.at[1 - core], gm_recv.at[turn, which])

    def marks(cell, slot):
        return meta[cell, pl.ds(slot, 1), :]

    def spread_users(turn):
        panel = panels[turn][ITEMS]
        for cell in range(2):
            for slot in range(SLOTS):
                rows = panel[meta_smem[cell, slot, 0] & 7].reshape(TILE, HALF)
                prod[cell * SLOTS + slot] = jnp.dot(
                    tiles[cell, slot], rows, preferred_element_type=F32
                )

        def add(number, carry):
            start = pl.ds(pl.multiple_of(lax.rem(number, 4) * ROWS, ROWS), ROWS)
            for cell in range(2):
                total = jnp.zeros((ROWS, HALF), F32)
                for slot in range(SLOTS):
                    weight = jnp.where((marks(cell, slot) >> 3) == number // 4, 1.0, 0.0)
                    total += weight.astype(F32) * prod[cell * SLOTS + slot, start, :]
                exact[USERS, number, cell] = total
                sums[turn, USERS, number, cell] = total.astype(BF16)
            return carry

        lax.fori_loop(0, BLOCKS, add, 0, unroll=4)

    def spread_items(turn):
        panel = panels[turn][USERS]
        for cell in range(2):
            for slot in range(SLOTS):
                tile = (meta_smem[cell, slot, 0] >> 3) & 3
                rows = panel[tile, :, cell].reshape(TILE, HALF)
                prod[cell * SLOTS + slot] = jnp.dot(
                    tiles_t[cell, slot], rows, preferred_element_type=F32
                )

        def add(number, carry):
            for owner in range(2):
                start = (lax.rem(number, 2) * 2 + owner) * ROWS
                start = pl.ds(pl.multiple_of(start, ROWS), ROWS)
                total = jnp.zeros((ROWS, HALF), F32)
                for cell in range(2):
                    for slot in range(SLOTS):
                        weight = jnp.where((marks(cell, slot) & 71) == number // 2, 1.0, 0.0)
                        total += weight.astype(F32) * prod[cell * SLOTS + slot, start, :]
                exact[ITEMS, number, owner] = total
                sums[turn, ITEMS, number, owner] = total.astype(BF16)
            return carry

        lax.fori_loop(0, BLOCKS, add, 0, unroll=4)

    def scatter_start(turn, which):
        out = s_send.at[turn, which]
        for other in (True, False):
            e = int(other)
            for way, step in ((0, 1), (1, -1)):
                sem = sf_recv.at[turn, which, e, way]
                send(sums.at[turn, which, block(which, other, 4), way],
                     far.at[turn, which, e, way, 2], out, sem, along(which, 2 * step))
                send(sums.at[turn, which, block(which, other, 3 * step)],
                     far.at[turn, which, e, way, pl.ds(0, 2)], out, sem, along(which, step))
        for way, step in ((0, 1), (1, -1)):
            send(sums.at[turn, which, block(which, True, step)], cross.at[turn, which, way],
                 out, sx_recv.at[turn, which], device(which, True, 0, core))
        for to_core in range(2):
            send_last(turn, which, True, 0, 5, to_core,
                      sums.at[turn, which, block(which, True, 0), to_core])
        send(sums.at[turn, which, block(which, False, 0), 1 - core],
             last.at[turn, which, core * 8], sm_send.at[turn, which], sl_recv.at[turn, which], mate)

    def send_last(turn, which, other, step, part, to_core, source):
        send(source, last.at[turn, which, core * 8 + part],
             s_send.at[turn, which], sl_recv.at[turn, which], device(which, other, step, to_core))

    def scatter_near(turn, which):
        awaits(cross.at[turn, which], sx_recv.at[turn, which])
        for way, step in ((0, 1), (1, -1)):
            number = block(which, False, step)
            for to_core in range(2):
                total = exact[which, number, to_core] + cross[turn, which, way, to_core].astype(F32)
                paired[turn, which, way, to_core] = total.astype(BF16)
            for to_core in range(2):
                send_last(turn, which, False, step, 1 + way, to_core,
                          paired.at[turn, which, way, to_core])

    def scatter_relay(turn, which, other):
        e = int(other)
        for way, step in ((0, 1), (1, -1)):
            came = far.at[turn, which, e, way]
            awaits(came, sf_recv.at[turn, which, e, way])
            mine = exact.at[which, block(which, other, 2 * step)]
            for owner in range(2):
                total = mine[owner] + came[owner].astype(F32)
                if owner == way:
                    total += came[2].astype(F32)
                relayed[turn, which, e, way, owner] = total.astype(BF16)
            for to_core in range(2):
                send_last(turn, which, other, 2 * step, (6 if other else 3) + way, to_core,
                          relayed.at[turn, which, e, way, to_core])

    def scatter_end(turn, which):
        awaits(last.at[turn, which, pl.ds(0, 15)], sl_recv.at[turn, which])
        last[turn, which, core * 8] = jnp.zeros((ROWS, HALF), BF16)
        own = exact[which, block(which, False, 0), core]
        sides = []
        for side in range(2):
            total = jnp.where(core == side, own, 0.0)
            for part in range(8):
                total += last[turn, which, side * 8 + part].astype(F32)
            sides.append(total)
        return jnp.concatenate(sides, axis=1)

    def prepare():
        user_base = (row * BLOCKS + col) * ROWS
        item_base = (col * 2 * BLOCKS + row) * ROWS
        places = lax.broadcasted_iota(jnp.int32, (ROWS, uid_ref.shape[1]), 0)
        hot = jnp.where(places == uid_ref[...] - user_base, 1.0, 0.0).astype(F32)
        user_hot[...] = hot.astype(BF16)
        user_hot_t[...] = jnp.concatenate([hot] * 3, axis=0).T.astype(BF16)
        hot = jnp.where(places == nid_ref[...] - item_base, 1.0, 0.0).astype(F32)
        hot = hot - jnp.where(places == pid_ref[...] - item_base, 1.0, 0.0).astype(F32)
        item_hot[...] = hot.astype(BF16)
        item_hot_t[...] = jnp.concatenate([hot] * 3, axis=0).T.astype(BF16)

    def gather_sent(turn):
        for which in (USERS, ITEMS):
            sent(stage.at[turn, which, core], gm_send.at[turn, which])
            sent(sums.at[turn, which, pl.ds(0, 15)], gb_send.at[turn, which])

    def scatter_sent(turn):
        for which in (USERS, ITEMS):
            sent(sums.at[turn, which, pl.ds(0, 15)], s_send.at[turn, which])
            sent(stage.at[turn, which, core], sm_send.at[turn, which])

    both = (ITEMS, USERS)

    def propagate(turn):
        if turn == 0:
            send(tiles_hbm, tiles.at[core], tile_send, tile_recv, mate)
            send(meta.at[core], meta.at[core], meta_send, meta_recv, mate)
            for copy in ids_load:
                copy.wait()
            prepare()
        for which in both:
            gather_relay(turn, which, False)
        for which in both:
            gather_cross(turn, which)
        for which in both:
            gather_relay(turn, which, True)
        if turn == 1:
            sent(tiles_hbm, tile_send)
            sent(meta.at[core], meta_send)
            gather_sent(0)
            scatter_sent(0)
        if turn == 0:
            tiles_load.wait()
            awaits(meta.at[1 - core], meta_recv)
            fill = pltpu.make_async_copy(meta, meta_smem, meta_sem)
            fill.start()
            fill.wait()
            awaits(tiles.at[1 - core], tile_recv)
            for cell in range(2):
                for slot in range(SLOTS):
                    tiles_t[cell, slot] = tiles[cell, slot].T
        gather_end(turn, ITEMS)
        spread_users(turn)
        scatter_start(turn, USERS)
        gather_end(turn, USERS)
        spread_items(turn)
        scatter_start(turn, ITEMS)
        for other in (True, False):
            for which in (USERS, ITEMS):
                scatter_relay(turn, which, other)
        for which in (USERS, ITEMS):
            scatter_near(turn, which)
        if turn == 1:
            gather_sent(1)

    items_load.wait()
    own_rows(0, ITEMS, items_ref[...])
    users_load.wait()
    own_rows(0, USERS, users_ref[...])
    pl.semaphore_wait(barrier, len(peers))
    for which in both:
        gather_start(0, which)
    propagate(0)
    dot = functools.partial(jnp.dot, preferred_element_type=F32)
    final_users = 0.5 * (users_ref[...] + scatter_end(0, USERS))
    chosen = dot(user_hot_t[...], split(final_users, 3))
    final_items = 0.5 * (items_ref[...] + scatter_end(0, ITEMS))
    against = dot(item_hot_t[...], split(final_items, 3))
    score = -jnp.sum(chosen * against, axis=1, keepdims=True)
    back = jax.nn.sigmoid(-score)
    hot = user_hot[...]
    grad_users = dot(jnp.concatenate([hot] * 2, axis=1), split(back * against, 2))
    own_rows(1, USERS, grad_users)
    gather_start(1, USERS)
    hot = item_hot[...]
    grad_items = dot(jnp.concatenate([hot] * 2, axis=1), split(back * chosen, 2))
    own_rows(1, ITEMS, grad_items)
    gather_start(1, ITEMS)
    propagate(1)
    out_ref[0] = 0.5 * grad_users + 0.5 * scatter_end(1, USERS)
    out_ref[1] = 0.5 * grad_items + 0.5 * scatter_end(1, ITEMS)
    scatter_sent(1)


def in_hbm(value):
    return pltpu.with_memory_space_constraint(value, pltpu.HBM)


def on_device(users, items, tiles, tile_pos, tile_count, user_ids, pos_ids, neg_ids):
    vmem = pl.BlockSpec(memory_space=pltpu.VMEM)
    dma = pltpu.SemaphoreType.DMA
    batch = user_ids.shape[0]
    cut = (2, ROWS, HALF)
    out = pl.pallas_call(
        kernel,
        out_shape=jax.ShapeDtypeStruct((2, ROWS, WIDTH), F32),
        in_specs=[pl.BlockSpec(memory_space=pl.ANY)] * 8,
        out_specs=vmem,
        scratch_shapes=[
            pltpu.VMEM((ROWS, WIDTH), F32),
            pltpu.VMEM((ROWS, WIDTH), F32),
            pltpu.SMEM((1, SLOTS), jnp.int32),
            pltpu.SMEM((1, 1), jnp.int32),
            pltpu.VMEM((1, batch), jnp.int32),
            pltpu.VMEM((1, batch), jnp.int32),
            pltpu.VMEM((1, batch), jnp.int32),
            pltpu.VMEM((2, SLOTS, TILE, TILE), BF16),
            pltpu.VMEM((2, SLOTS, TILE, TILE), BF16),
            pltpu.VMEM((2, 8, HALF), jnp.int32),
            pltpu.SMEM((2, 8, HALF), jnp.int32),
            pltpu.VMEM((ROWS, batch), BF16),
            pltpu.VMEM((ROWS, batch), BF16),
            pltpu.VMEM((batch, 3 * ROWS), BF16),
            pltpu.VMEM((batch, 3 * ROWS), BF16),
            pltpu.VMEM((4, 4) + cut, BF16),
            pltpu.VMEM((4, 4) + cut, BF16),
            pltpu.VMEM((8, 2) + cut, BF16),
            pltpu.VMEM((8, 2) + cut, BF16),
            pltpu.VMEM((2, 2) + cut, BF16),
            pltpu.VMEM((2 * SLOTS, TILE, HALF), F32),
            pltpu.VMEM((2, BLOCKS) + cut, F32),
            pltpu.VMEM((2, 2, BLOCKS) + cut, BF16),
            pltpu.VMEM((2, 2, 2, 2, 3, ROWS, HALF), BF16),
            pltpu.VMEM((2, 2, 2) + cut, BF16),
            pltpu.VMEM((2, 2, 2) + cut, BF16),
            pltpu.VMEM((2, 2, 2, 2) + cut, BF16),
            pltpu.VMEM((2, 2, 16, ROWS, HALF), BF16),
            dma((8,)),
            dma,
            dma,
            dma,
            dma,
            dma,
            dma((2, 2)),
            dma((2, 2)),
            dma((2, 2, 2)),
            dma((2, 2, 2, 2)),
            dma((2, 2)),
            dma((2, 2)),
            dma((2, 2, 2, 2)),
            dma((2, 2)),
            dma((2, 2)),
            dma((2, 2)),
            dma((2, 2)),
        ],
        compiler_params=pltpu.CompilerParams(
            collective_id=0, has_side_effects=True, vmem_limit_bytes=40 << 20
        ),
        name="propagation_layer",
    )(
        in_hbm(users),
        in_hbm(items),
        in_hbm(tile_pos.reshape(1, SLOTS)),
        tile_count,
        in_hbm(user_ids.reshape(1, batch)),
        in_hbm(pos_ids.reshape(1, batch)),
        in_hbm(neg_ids.reshape(1, batch)),
        in_hbm(tiles.reshape(SLOTS, TILE, TILE)),
    )
    return out[0], out[1]


def solution(mesh):
    placed = (
        P(("row", "col"), None),
        P(("col", "row"), None),
        P("row", "col", None, None, None),
        P("row", "col", None),
        P("row", "col"),
        P(("row", "col")),
        P(("row", "col")),
        P(("row", "col")),
    )
    return jax.shard_map(
        on_device,
        mesh=mesh,
        in_specs=placed,
        out_specs=(P(("row", "col"), None), P(("col", "row"), None)),
        check_vma=False,
    )
```

```python
import functools

import jax
import jax.numpy as jnp
from jax import lax
from jax.experimental import pallas as pl
from jax.experimental.pallas import tpu as pltpu
from jax.sharding import PartitionSpec as P

MESH = pl.DeviceIdType.MESH
BF16 = jnp.bfloat16
F32 = jnp.float32
SLOTS = 4
ROWS = 64
HALF = 128
WIDTH = 256
TILE = 256
RING = 8
BLOCKS = 16
USERS, ITEMS = 0, 1


def split(value, parts):
    terms = []
    for part in range(parts):
        term = value.astype(BF16)
        terms.append(term)
        value = value - term.astype(F32)
    return jnp.concatenate(terms, axis=0)


def kernel(
    users_hbm,
    items_hbm,
    pos_hbm,
    count_hbm,
    uid_hbm,
    pid_hbm,
    nid_hbm,
    tiles_hbm,
    out_ref,
    users_ref,
    items_ref,
    pos_ref,
    count_ref,
    uid_ref,
    pid_ref,
    nid_ref,
    tiles,
    tiles_t,
    meta,
    meta_smem,
    user_hot,
    item_hot,
    user_hot_t,
    item_hot_t,
    user_panel_0,
    user_panel_1,
    item_panel_0,
    item_panel_1,
    stage,
    prod,
    exact,
    sums,
    far,
    cross,
    paired,
    relayed,
    last,
    load_sem,
    tile_send,
    tile_recv,
    meta_sem,
    meta_send,
    meta_recv,
    gm_send,
    gm_recv,
    g1_recv,
    g2_recv,
    gb_send,
    gb_recv,
    sf_recv,
    sx_recv,
    sl_recv,
    s_send,
    sm_send,
):
    row = lax.axis_index("row")
    col = lax.axis_index("col")
    core = lax.rem(row, 2)
    group = row // 2
    mate = (row + 1 - 2 * core, col)
    x_at = (col // RING, group // RING)
    ring_at = (lax.rem(col, RING), lax.rem(group, RING))

    def block(which, other, step):
        x = 1 - x_at[which] if other else x_at[which]
        return x * RING + lax.rem(ring_at[which] + step + RING, RING)

    def device(which, other, step, to_core):
        number = block(which, other, step)
        if which == USERS:
            return (group * 2 + to_core, number)
        return (number * 2 + to_core, col)

    def along(which, step):
        return device(which, False, step, core)

    def send(source, target, send_sem, recv_sem, to):
        pltpu.make_async_remote_copy(
            src_ref=source, dst_ref=target, send_sem=send_sem, recv_sem=recv_sem,
            device_id=to, device_id_type=MESH,
        ).start()

    def awaits(ref, sem):
        pltpu.make_async_remote_copy(
            src_ref=ref, dst_ref=ref, send_sem=sem, recv_sem=sem,
            device_id=mate, device_id_type=MESH,
        ).wait_recv()

    def sent(ref, sem):
        pltpu.make_async_remote_copy(
            src_ref=ref, dst_ref=ref, send_sem=sem, recv_sem=sem,
            device_id=mate, device_id_type=MESH,
        ).wait_send()

    def load(number, source, target):
        copy = pltpu.make_async_copy(source, target, load_sem.at[number])
        copy.start()
        return copy

    barrier = pltpu.get_barrier_semaphore()
    far_steps = [(other, step) for step in (2, -2) for other in (True, False)]
    near_steps = [(False, 1), (False, -1), (True, 0)]
    peers = [mate]
    for which in (USERS, ITEMS):
        for other, step in far_steps + near_steps:
            peers += [device(which, other, step, to_core) for to_core in range(2)]
    for peer in peers:
        pl.semaphore_signal(barrier, 1, device_id=peer, device_id_type=MESH)

    items_load = load(0, items_hbm, items_ref)
    users_load = load(1, users_hbm, users_ref)
    pos_load = load(2, pos_hbm, pos_ref)
    count_load = load(3, count_hbm, count_ref)
    ids_load = [
        load(4, uid_hbm, uid_ref), load(5, pid_hbm, pid_ref), load(6, nid_hbm, nid_ref)
    ]
    tiles_load = load(7, tiles_hbm, tiles.at[core])

    pos_load.wait()
    count_load.wait()
    filled = jnp.full((8, HALF), count_ref[0, 0], jnp.int32)
    slot_of = lax.broadcasted_iota(jnp.int32, (8, HALF), 0)
    placed = jnp.full((8, HALF), pos_ref[0, 0], jnp.int32)
    for slot in range(1, SLOTS):
        placed = jnp.where(slot_of == slot, jnp.full((8, HALF), pos_ref[0, slot], jnp.int32), placed)
    meta[core] = jnp.where(slot_of < filled, placed, placed + 64)

    panels = ((user_panel_0, item_panel_0), (user_panel_1, item_panel_1))

    def at_block(turn, which, number):
        per = 4 if which == USERS else 2
        return panels[turn][which].at[number // per, lax.rem(number, per)]

    def own_rows(turn, which, value):
        stage[turn, which, 0] = value[:, :HALF].astype(BF16)
        stage[turn, which, 1] = value[:, HALF:].astype(BF16)
        own = at_block(turn, which, block(which, False, 0))
        own[core] = stage[turn, which, core]

    def gather_start(turn, which):
        own = at_block(turn, which, block(which, False, 0)).at[core]
        for other, step in far_steps + near_steps:
            if abs(step) == 2:
                sem = g2_recv.at[turn, which, int(other), int(step < 0)]
            elif abs(step) == 1:
                sem = g1_recv.at[turn, which, int(step < 0)]
            else:
                sem = gb_recv.at[turn, which]
            for to_core in range(2):
                send(stage.at[turn, which, to_core], own, gb_send.at[turn, which], sem,
                     device(which, other, step, to_core))
        send(stage.at[turn, which, 1 - core], own,
             gm_send.at[turn, which], gm_recv.at[turn, which], mate)

    def gather_relay(turn, which, other):
        for way, step in ((0, 1), (1, -1)):
            here = at_block(turn, which, block(which, other, -2 * step))
            awaits(here, g2_recv.at[turn, which, int(other), way])
            part = here.at[way]
            send(part, part, gb_send.at[turn, which], gb_recv.at[turn, which], along(which, 2 * step))
            send(here, here, gb_send.at[turn, which], gb_recv.at[turn, which], along(which, step))

    def gather_cross(turn, which):
        for way, step in ((0, 1), (1, -1)):
            here = at_block(turn, which, block(which, False, -step))
            awaits(here, g1_recv.at[turn, which, way])
            send(here, here, gb_send.at[turn, which], gb_recv.at[turn, which],
                 device(which, True, 0, core))

    def gather_end(turn, which):
        awaits(sums.at[turn, which, pl.ds(0, 9)], gb_recv.at[turn, which])
        own = at_block(turn, which, block(which, False, 0))
        awaits(own.at[1 - core], gm_recv.at[turn, which])

    def marks(cell, slot):
        return meta[cell, pl.ds(slot, 1), :]

    def products(turn, which):
        panel = panels[turn][1 - which]
        for cell in range(2):
            for slot in range(SLOTS):
                place = meta_smem[cell, slot, 0]
                if which == USERS:
                    rows, left = panel[place & 7], tiles[cell, slot]
                else:
                    rows, left = panel[(place >> 3) & 3, :, cell], tiles_t[cell, slot]
                prod[which, cell * SLOTS + slot] = jnp.dot(
                    left, rows.reshape(TILE, HALF), preferred_element_type=F32
                )

    def add_users(number):
        start = pl.ds(pl.multiple_of(lax.rem(number, 4) * ROWS, ROWS), ROWS)
        for cell in range(2):
            total = jnp.zeros((ROWS, HALF), F32)
            for slot in range(SLOTS):
                weight = jnp.where((marks(cell, slot) >> 3) == number // 4, 1.0, 0.0)
                total += weight.astype(F32) * prod[USERS, cell * SLOTS + slot, start, :]
            yield cell, total

    def add_items(number):
        for owner in range(2):
            start = (lax.rem(number, 2) * 2 + owner) * ROWS
            start = pl.ds(pl.multiple_of(start, ROWS), ROWS)
            total = jnp.zeros((ROWS, HALF), F32)
            for cell in range(2):
                for slot in range(SLOTS):
                    weight = jnp.where((marks(cell, slot) & 71) == number // 2, 1.0, 0.0)
                    total += weight.astype(F32) * prod[ITEMS, cell * SLOTS + slot, start, :]
            yield owner, total

    def sum_blocks(turn, which, first, count):
        def add(index, carry):
            x = lax.rem(x_at[which] + 1 - index // count, 2)
            along_ring = lax.rem(ring_at[which] + first + lax.rem(index, count), RING)
            number = x * RING + along_ring
            for part, total in (add_users if which == USERS else add_items)(number):
                exact[which, number, part] = total
                sums[turn, which, number, part] = total.astype(BF16)
            return carry

        lax.fori_loop(0, 2 * count, add, 0, unroll=count)

    def scatter_far(turn, which):
        out = s_send.at[turn, which]
        for other in (True, False):
            e = int(other)
            for way, step in ((0, 1), (1, -1)):
                sem = sf_recv.at[turn, which, e, way]
                send(sums.at[turn, which, block(which, other, 4), way],
                     far.at[turn, which, e, way, 2], out, sem, along(which, 2 * step))
                send(sums.at[turn, which, block(which, other, 3 * step)],
                     far.at[turn, which, e, way, pl.ds(0, 2)], out, sem, along(which, step))

    def scatter_rest(turn, which):
        out = s_send.at[turn, which]
        for way, step in ((0, 1), (1, -1)):
            send(sums.at[turn, which, block(which, True, step)], cross.at[turn, which, way],
                 out, sx_recv.at[turn, which], device(which, True, 0, core))
        for to_core in range(2):
            send_last(turn, which, True, 0, 5, to_core,
                      sums.at[turn, which, block(which, True, 0), to_core])
        send(sums.at[turn, which, block(which, False, 0), 1 - core],
             last.at[turn, which, core * 8], sm_send.at[turn, which], sl_recv.at[turn, which], mate)

    def send_last(turn, which, other, step, part, to_core, source):
        send(source, last.at[turn, which, core * 8 + part],
             s_send.at[turn, which], sl_recv.at[turn, which], device(which, other, step, to_core))

    def scatter_near(turn, which):
        awaits(cross.at[turn, which], sx_recv.at[turn, which])
        for way, step in ((0, 1), (1, -1)):
            number = block(which, False, step)
            for to_core in range(2):
                total = exact[which, number, to_core] + cross[turn, which, way, to_core].astype(F32)
                paired[turn, which, way, to_core] = total.astype(BF16)
            for to_core in range(2):
                send_last(turn, which, False, step, 1 + way, to_core,
                          paired.at[turn, which, way, to_core])

    def scatter_relay(turn, which, other):
        e = int(other)
        for way, step in ((0, 1), (1, -1)):
            came = far.at[turn, which, e, way]
            awaits(came, sf_recv.at[turn, which, e, way])
            mine = exact.at[which, block(which, other, 2 * step)]
            for owner in range(2):
                total = mine[owner] + came[owner].astype(F32)
                if owner == way:
                    total += came[2].astype(F32)
                relayed[turn, which, e, way, owner] = total.astype(BF16)
            for to_core in range(2):
                send_last(turn, which, other, 2 * step, (6 if other else 3) + way, to_core,
                          relayed.at[turn, which, e, way, to_core])

    def scatter_end(turn, which):
        awaits(last.at[turn, which, pl.ds(0, 15)], sl_recv.at[turn, which])
        last[turn, which, core * 8] = jnp.zeros((ROWS, HALF), BF16)
        own = exact[which, block(which, False, 0), core]
        sides = []
        for side in range(2):
            total = jnp.where(core == side, own, 0.0)
            for part in range(8):
                total += last[turn, which, side * 8 + part].astype(F32)
            sides.append(total)
        return jnp.concatenate(sides, axis=1)

    def prepare():
        user_base = (row * BLOCKS + col) * ROWS
        item_base = (col * 2 * BLOCKS + row) * ROWS
        places = lax.broadcasted_iota(jnp.int32, (ROWS, uid_ref.shape[1]), 0)
        hot = jnp.where(places == uid_ref[...] - user_base, 1.0, 0.0).astype(F32)
        user_hot[...] = hot.astype(BF16)
        user_hot_t[...] = jnp.concatenate([hot] * 3, axis=0).T.astype(BF16)
        hot = jnp.where(places == nid_ref[...] - item_base, 1.0, 0.0).astype(F32)
        hot = hot - jnp.where(places == pid_ref[...] - item_base, 1.0, 0.0).astype(F32)
        item_hot[...] = hot.astype(BF16)
        item_hot_t[...] = jnp.concatenate([hot] * 3, axis=0).T.astype(BF16)

    def gather_sent(turn):
        for which in (USERS, ITEMS):
            sent(stage.at[turn, which, core], gm_send.at[turn, which])
            sent(sums.at[turn, which, pl.ds(0, 15)], gb_send.at[turn, which])

    def scatter_sent(turn):
        for which in (USERS, ITEMS):
            sent(sums.at[turn, which, pl.ds(0, 15)], s_send.at[turn, which])
            sent(stage.at[turn, which, core], sm_send.at[turn, which])

    both = (ITEMS, USERS)

    def propagate(turn):
        if turn == 0:
            send(tiles_hbm, tiles.at[core], tile_send, tile_recv, mate)
            send(meta.at[core], meta.at[core], meta_send, meta_recv, mate)
            for copy in ids_load:
                copy.wait()
            prepare()
        for which in both:
            gather_relay(turn, which, False)
        for which in both:
            gather_cross(turn, which)
        for which in both:
            gather_relay(turn, which, True)
        if turn == 1:
            sent(tiles_hbm, tile_send)
            sent(meta.at[core], meta_send)
            gather_sent(0)
            scatter_sent(0)
        if turn == 0:
            tiles_load.wait()
            awaits(meta.at[1 - core], meta_recv)
            fill = pltpu.make_async_copy(meta, meta_smem, meta_sem)
            fill.start()
            fill.wait()
            awaits(tiles.at[1 - core], tile_recv)
            for cell in range(2):
                for slot in range(SLOTS):
                    tiles_t[cell, slot] = tiles[cell, slot].T
        for which in (USERS, ITEMS):
            gather_end(turn, 1 - which)
            products(turn, which)
            sum_blocks(turn, which, 3, 3)
            scatter_far(turn, which)
        for which in (USERS, ITEMS):
            sum_blocks(turn, which, 6, 5)
            scatter_rest(turn, which)
        for other in (True, False):
            for which in (USERS, ITEMS):
                scatter_relay(turn, which, other)
        for which in (USERS, ITEMS):
            scatter_near(turn, which)
        if turn == 1:
            gather_sent(1)

    items_load.wait()
    own_rows(0, ITEMS, items_ref[...])
    users_load.wait()
    own_rows(0, USERS, users_ref[...])
    pl.semaphore_wait(barrier, len(peers))
    for which in both:
        gather_start(0, which)
    propagate(0)
    dot = functools.partial(jnp.dot, preferred_element_type=F32)
    final_users = 0.5 * (users_ref[...] + scatter_end(0, USERS))
    chosen = dot(user_hot_t[...], split(final_users, 3))
    final_items = 0.5 * (items_ref[...] + scatter_end(0, ITEMS))
    against = dot(item_hot_t[...], split(final_items, 3))
    score = -jnp.sum(chosen * against, axis=1, keepdims=True)
    back = jax.nn.sigmoid(-score)
    hot = user_hot[...]
    grad_users = dot(jnp.concatenate([hot] * 2, axis=1), split(back * against, 2))
    own_rows(1, USERS, grad_users)
    gather_start(1, USERS)
    hot = item_hot[...]
    grad_items = dot(jnp.concatenate([hot] * 2, axis=1), split(back * chosen, 2))
    own_rows(1, ITEMS, grad_items)
    gather_start(1, ITEMS)
    propagate(1)
    out_ref[0] = 0.5 * grad_users + 0.5 * scatter_end(1, USERS)
    out_ref[1] = 0.5 * grad_items + 0.5 * scatter_end(1, ITEMS)
    scatter_sent(1)


def in_hbm(value):
    return pltpu.with_memory_space_constraint(value, pltpu.HBM)


def on_device(users, items, tiles, tile_pos, tile_count, user_ids, pos_ids, neg_ids):
    vmem = pl.BlockSpec(memory_space=pltpu.VMEM)
    dma = pltpu.SemaphoreType.DMA
    batch = user_ids.shape[0]
    cut = (2, ROWS, HALF)
    out = pl.pallas_call(
        kernel,
        out_shape=jax.ShapeDtypeStruct((2, ROWS, WIDTH), F32),
        in_specs=[pl.BlockSpec(memory_space=pl.ANY)] * 8,
        out_specs=vmem,
        scratch_shapes=[
            pltpu.VMEM((ROWS, WIDTH), F32),
            pltpu.VMEM((ROWS, WIDTH), F32),
            pltpu.SMEM((1, SLOTS), jnp.int32),
            pltpu.SMEM((1, 1), jnp.int32),
            pltpu.VMEM((1, batch), jnp.int32),
            pltpu.VMEM((1, batch), jnp.int32),
            pltpu.VMEM((1, batch), jnp.int32),
            pltpu.VMEM((2, SLOTS, TILE, TILE), BF16),
            pltpu.VMEM((2, SLOTS, TILE, TILE), BF16),
            pltpu.VMEM((2, 8, HALF), jnp.int32),
            pltpu.SMEM((2, 8, HALF), jnp.int32),
            pltpu.VMEM((ROWS, batch), BF16),
            pltpu.VMEM((ROWS, batch), BF16),
            pltpu.VMEM((batch, 3 * ROWS), BF16),
            pltpu.VMEM((batch, 3 * ROWS), BF16),
            pltpu.VMEM((4, 4) + cut, BF16),
            pltpu.VMEM((4, 4) + cut, BF16),
            pltpu.VMEM((8, 2) + cut, BF16),
            pltpu.VMEM((8, 2) + cut, BF16),
            pltpu.VMEM((2, 2) + cut, BF16),
            pltpu.VMEM((2, 2 * SLOTS, TILE, HALF), F32),
            pltpu.VMEM((2, BLOCKS) + cut, F32),
            pltpu.VMEM((2, 2, BLOCKS) + cut, BF16),
            pltpu.VMEM((2, 2, 2, 2, 3, ROWS, HALF), BF16),
            pltpu.VMEM((2, 2, 2) + cut, BF16),
            pltpu.VMEM((2, 2, 2) + cut, BF16),
            pltpu.VMEM((2, 2, 2, 2) + cut, BF16),
            pltpu.VMEM((2, 2, 16, ROWS, HALF), BF16),
            dma((8,)),
            dma,
            dma,
            dma,
            dma,
            dma,
            dma((2, 2)),
            dma((2, 2)),
            dma((2, 2, 2)),
            dma((2, 2, 2, 2)),
            dma((2, 2)),
            dma((2, 2)),
            dma((2, 2, 2, 2)),
            dma((2, 2)),
            dma((2, 2)),
            dma((2, 2)),
            dma((2, 2)),
        ],
        compiler_params=pltpu.CompilerParams(
            collective_id=0, has_side_effects=True, vmem_limit_bytes=40 << 20
        ),
        name="propagation_layer",
    )(
        in_hbm(users),
        in_hbm(items),
        in_hbm(tile_pos.reshape(1, SLOTS)),
        tile_count,
        in_hbm(user_ids.reshape(1, batch)),
        in_hbm(pos_ids.reshape(1, batch)),
        in_hbm(neg_ids.reshape(1, batch)),
        in_hbm(tiles.reshape(SLOTS, TILE, TILE)),
    )
    return out[0], out[1]


def solution(mesh):
    placed = (
        P(("row", "col"), None),
        P(("col", "row"), None),
        P("row", "col", None, None, None),
        P("row", "col", None),
        P("row", "col"),
        P(("row", "col")),
        P(("row", "col")),
        P(("row", "col")),
    )
    return jax.shard_map(
        on_device,
        mesh=mesh,
        in_specs=placed,
        out_specs=(P(("row", "col"), None), P(("col", "row"), None)),
        check_vma=False,
    )
```

```python
import functools

import jax
import jax.numpy as jnp
from jax import lax
from jax.experimental import pallas as pl
from jax.experimental.pallas import tpu as pltpu
from jax.sharding import PartitionSpec as P

MESH = pl.DeviceIdType.MESH
BF16 = jnp.bfloat16
F32 = jnp.float32
SLOTS = 4
ROWS = 64
HALF = 128
WIDTH = 256
TILE = 256
RING = 8
BLOCKS = 16
USERS, ITEMS = 0, 1


def split(value, parts):
    terms = []
    for part in range(parts):
        term = value.astype(BF16)
        terms.append(term)
        value = value - term.astype(F32)
    return jnp.concatenate(terms, axis=0)


def kernel(
    users_hbm,
    items_hbm,
    pos_hbm,
    count_hbm,
    uid_hbm,
    pid_hbm,
    nid_hbm,
    tiles_hbm,
    out_ref,
    users_ref,
    items_ref,
    pos_ref,
    count_ref,
    uid_ref,
    pid_ref,
    nid_ref,
    tiles,
    tiles_t,
    meta,
    meta_smem,
    user_hot,
    item_hot,
    user_hot_t,
    item_hot_t,
    user_panel_0,
    user_panel_1,
    item_panel_0,
    item_panel_1,
    stage,
    prod,
    exact,
    sums,
    far,
    cross,
    paired,
    relayed,
    last,
    load_sem,
    tile_send,
    tile_recv,
    meta_sem,
    meta_send,
    meta_recv,
    gm_send,
    gm_recv,
    g1_recv,
    g2_recv,
    gb_send,
    gb_recv,
    sf_recv,
    sx_recv,
    sl_recv,
    s_send,
    sm_send,
):
    row = lax.axis_index("row")
    col = lax.axis_index("col")
    core = lax.rem(row, 2)
    group = row // 2
    mate = (row + 1 - 2 * core, col)
    x_at = (col // RING, group // RING)
    ring_at = (lax.rem(col, RING), lax.rem(group, RING))

    def block(which, other, step):
        x = 1 - x_at[which] if other else x_at[which]
        return x * RING + lax.rem(ring_at[which] + step + RING, RING)

    def device(which, other, step, to_core):
        number = block(which, other, step)
        if which == USERS:
            return (group * 2 + to_core, number)
        return (number * 2 + to_core, col)

    def along(which, step):
        return device(which, False, step, core)

    def send(source, target, send_sem, recv_sem, to):
        pltpu.make_async_remote_copy(
            src_ref=source, dst_ref=target, send_sem=send_sem, recv_sem=recv_sem,
            device_id=to, device_id_type=MESH,
        ).start()

    def awaits(ref, sem):
        pltpu.make_async_remote_copy(
            src_ref=ref, dst_ref=ref, send_sem=sem, recv_sem=sem,
            device_id=mate, device_id_type=MESH,
        ).wait_recv()

    def sent(ref, sem):
        pltpu.make_async_remote_copy(
            src_ref=ref, dst_ref=ref, send_sem=sem, recv_sem=sem,
            device_id=mate, device_id_type=MESH,
        ).wait_send()

    def load(number, source, target):
        copy = pltpu.make_async_copy(source, target, load_sem.at[number])
        copy.start()
        return copy

    barrier = pltpu.get_barrier_semaphore()
    far_steps = [(other, step) for step in (2, -2) for other in (True, False)]
    near_steps = [(False, 1), (False, -1), (True, 0)]
    peers = [mate]
    for which in (USERS, ITEMS):
        for other, step in far_steps + near_steps:
            peers += [device(which, other, step, to_core) for to_core in range(2)]
    for peer in peers:
        pl.semaphore_signal(barrier, 1, device_id=peer, device_id_type=MESH)

    items_load = load(0, items_hbm, items_ref)
    users_load = load(1, users_hbm, users_ref)
    pos_load = load(2, pos_hbm, pos_ref)
    count_load = load(3, count_hbm, count_ref)
    ids_load = [
        load(4, uid_hbm, uid_ref), load(5, pid_hbm, pid_ref), load(6, nid_hbm, nid_ref)
    ]
    tiles_load = load(7, tiles_hbm, tiles.at[core])

    panels = ((user_panel_0, item_panel_0), (user_panel_1, item_panel_1))

    def at_block(turn, which, number):
        per = 4 if which == USERS else 2
        return panels[turn][which].at[number // per, lax.rem(number, per)]

    def own_rows(turn, which, value):
        stage[turn, which, 0] = value[:, :HALF].astype(BF16)
        stage[turn, which, 1] = value[:, HALF:].astype(BF16)
        own = at_block(turn, which, block(which, False, 0))
        own[core] = stage[turn, which, core]

    def gather_start(turn, which):
        own = at_block(turn, which, block(which, False, 0)).at[core]
        for other, step in far_steps + near_steps:
            if abs(step) == 2:
                sem = g2_recv.at[turn, which, int(other), int(step < 0)]
            elif abs(step) == 1:
                sem = g1_recv.at[turn, which, int(step < 0)]
            else:
                sem = gb_recv.at[turn, which]
            for to_core in range(2):
                send(stage.at[turn, which, to_core], own, gb_send.at[turn, which], sem,
                     device(which, other, step, to_core))
        send(stage.at[turn, which, 1 - core], own,
             gm_send.at[turn, which], gm_recv.at[turn, which], mate)

    def gather_relay(turn, which, other):
        for way, step in ((0, 1), (1, -1)):
            here = at_block(turn, which, block(which, other, -2 * step))
            awaits(here, g2_recv.at[turn, which, int(other), way])
            part = here.at[way]
            send(part, part, gb_send.at[turn, which], gb_recv.at[turn, which], along(which, 2 * step))
            send(here, here, gb_send.at[turn, which], gb_recv.at[turn, which], along(which, step))

    def gather_cross(turn, which):
        for way, step in ((0, 1), (1, -1)):
            here = at_block(turn, which, block(which, False, -step))
            awaits(here, g1_recv.at[turn, which, way])
            send(here, here, gb_send.at[turn, which], gb_recv.at[turn, which],
                 device(which, True, 0, core))

    def gather_end(turn, which):
        awaits(sums.at[turn, which, pl.ds(0, 9)], gb_recv.at[turn, which])
        own = at_block(turn, which, block(which, False, 0))
        awaits(own.at[1 - core], gm_recv.at[turn, which])

    def marks(cell, slot):
        return meta[cell, pl.ds(slot, 1), :]

    def spread_users(turn):
        panel = panels[turn][ITEMS]
        for cell in range(2):
            for slot in range(SLOTS):
                rows = panel[meta_smem[cell, slot, 0] & 7].reshape(TILE, HALF)
                prod[cell * SLOTS + slot] = jnp.dot(
                    tiles[cell, slot], rows, preferred_element_type=F32
                )

        def add(number, carry):
            start = pl.ds(pl.multiple_of(lax.rem(number, 4) * ROWS, ROWS), ROWS)
            for cell in range(2):
                total = jnp.zeros((ROWS, HALF), F32)
                for slot in range(SLOTS):
                    weight = jnp.where((marks(cell, slot) >> 3) == number // 4, 1.0, 0.0)
                    total += weight.astype(F32) * prod[cell * SLOTS + slot, start, :]
                exact[USERS, number, cell] = total
                sums[turn, USERS, number, cell] = total.astype(BF16)
            return carry

        lax.fori_loop(0, BLOCKS, add, 0, unroll=4)

    def spread_items(turn):
        panel = panels[turn][USERS]
        for cell in range(2):
            for slot in range(SLOTS):
                tile = (meta_smem[cell, slot, 0] >> 3) & 3
                rows = panel[tile, :, cell].reshape(TILE, HALF)
                prod[cell * SLOTS + slot] = jnp.dot(
                    tiles_t[cell, slot], rows, preferred_element_type=F32
                )

        def add(number, carry):
            for owner in range(2):
                start = (lax.rem(number, 2) * 2 + owner) * ROWS
                start = pl.ds(pl.multiple_of(start, ROWS), ROWS)
                total = jnp.zeros((ROWS, HALF), F32)
                for cell in range(2):
                    for slot in range(SLOTS):
                        weight = jnp.where((marks(cell, slot) & 71) == number // 2, 1.0, 0.0)
                        total += weight.astype(F32) * prod[cell * SLOTS + slot, start, :]
                exact[ITEMS, number, owner] = total
                sums[turn, ITEMS, number, owner] = total.astype(BF16)
            return carry

        lax.fori_loop(0, BLOCKS, add, 0, unroll=4)

    def scatter_start(turn, which):
        out = s_send.at[turn, which]
        for other in (True, False):
            e = int(other)
            for way, step in ((0, 1), (1, -1)):
                sem = sf_recv.at[turn, which, e, way]
                send(sums.at[turn, which, block(which, other, 4), way],
                     far.at[turn, which, e, way, 2], out, sem, along(which, 2 * step))
                send(sums.at[turn, which, block(which, other, 3 * step)],
                     far.at[turn, which, e, way, pl.ds(0, 2)], out, sem, along(which, step))
        for way, step in ((0, 1), (1, -1)):
            send(sums.at[turn, which, block(which, True, step)], cross.at[turn, which, way],
                 out, sx_recv.at[turn, which], device(which, True, 0, core))
        for to_core in range(2):
            send_last(turn, which, True, 0, 5, to_core,
                      sums.at[turn, which, block(which, True, 0), to_core])
        send(sums.at[turn, which, block(which, False, 0), 1 - core],
             last.at[turn, which, core * 8], sm_send.at[turn, which], sl_recv.at[turn, which], mate)

    def send_last(turn, which, other, step, part, to_core, source):
        send(source, last.at[turn, which, core * 8 + part],
             s_send.at[turn, which], sl_recv.at[turn, which], device(which, other, step, to_core))

    def scatter_near(turn, which):
        awaits(cross.at[turn, which], sx_recv.at[turn, which])
        for way, step in ((0, 1), (1, -1)):
            number = block(which, False, step)
            for to_core in range(2):
                total = exact[which, number, to_core] + cross[turn, which, way, to_core].astype(F32)
                paired[turn, which, way, to_core] = total.astype(BF16)
            for to_core in range(2):
                send_last(turn, which, False, step, 1 + way, to_core,
                          paired.at[turn, which, way, to_core])

    def scatter_relay(turn, which, other):
        e = int(other)
        for way, step in ((0, 1), (1, -1)):
            came = far.at[turn, which, e, way]
            awaits(came, sf_recv.at[turn, which, e, way])
            mine = exact.at[which, block(which, other, 2 * step)]
            for owner in range(2):
                total = mine[owner] + came[owner].astype(F32)
                if owner == way:
                    total += came[2].astype(F32)
                relayed[turn, which, e, way, owner] = total.astype(BF16)
            for to_core in range(2):
                send_last(turn, which, other, 2 * step, (6 if other else 3) + way, to_core,
                          relayed.at[turn, which, e, way, to_core])

    def scatter_end(turn, which):
        awaits(last.at[turn, which, pl.ds(0, 15)], sl_recv.at[turn, which])
        last[turn, which, core * 8] = jnp.zeros((ROWS, HALF), BF16)
        own = exact[which, block(which, False, 0), core]
        sides = []
        for side in range(2):
            total = jnp.where(core == side, own, 0.0)
            for part in range(8):
                total += last[turn, which, side * 8 + part].astype(F32)
            sides.append(total)
        return jnp.concatenate(sides, axis=1)

    def prepare():
        user_base = (row * BLOCKS + col) * ROWS
        item_base = (col * 2 * BLOCKS + row) * ROWS
        places = lax.broadcasted_iota(jnp.int32, (ROWS, uid_ref.shape[1]), 0)
        hot = jnp.where(places == uid_ref[...] - user_base, 1.0, 0.0).astype(F32)
        user_hot[...] = hot.astype(BF16)
        user_hot_t[...] = jnp.concatenate([hot] * 3, axis=0).T.astype(BF16)
        hot = jnp.where(places == nid_ref[...] - item_base, 1.0, 0.0).astype(F32)
        hot = hot - jnp.where(places == pid_ref[...] - item_base, 1.0, 0.0).astype(F32)
        item_hot[...] = hot.astype(BF16)
        item_hot_t[...] = jnp.concatenate([hot] * 3, axis=0).T.astype(BF16)

    def gather_sent(turn):
        for which in (USERS, ITEMS):
            sent(stage.at[turn, which, core], gm_send.at[turn, which])
            sent(sums.at[turn, which, pl.ds(0, 15)], gb_send.at[turn, which])

    def scatter_sent(turn):
        for which in (USERS, ITEMS):
            sent(sums.at[turn, which, pl.ds(0, 15)], s_send.at[turn, which])
            sent(stage.at[turn, which, core], sm_send.at[turn, which])

    both = (ITEMS, USERS)

    def propagate(turn):
        if turn == 0:
            send(tiles_hbm, tiles.at[core], tile_send, tile_recv, mate)
            send(meta.at[core], meta.at[core], meta_send, meta_recv, mate)
            for copy in ids_load:
                copy.wait()
            prepare()
        for which in both:
            gather_relay(turn, which, False)
        for which in both:
            gather_cross(turn, which)
        for which in both:
            gather_relay(turn, which, True)
        if turn == 1:
            sent(tiles_hbm, tile_send)
            sent(meta.at[core], meta_send)
            gather_sent(0)
            scatter_sent(0)
        if turn == 0:
            tiles_load.wait()
            awaits(meta.at[1 - core], meta_recv)
            fill = pltpu.make_async_copy(meta, meta_smem, meta_sem)
            fill.start()
            fill.wait()
            awaits(tiles.at[1 - core], tile_recv)
            for cell in range(2):
                for slot in range(SLOTS):
                    tiles_t[cell, slot] = tiles[cell, slot].T
        gather_end(turn, ITEMS)
        spread_users(turn)
        scatter_start(turn, USERS)
        gather_end(turn, USERS)
        spread_items(turn)
        scatter_start(turn, ITEMS)
        for other in (True, False):
            for which in (USERS, ITEMS):
                scatter_relay(turn, which, other)
        for which in (USERS, ITEMS):
            scatter_near(turn, which)
        if turn == 1:
            gather_sent(1)

    items_load.wait()
    own_rows(0, ITEMS, items_ref[...])
    pl.semaphore_wait(barrier, len(peers))
    gather_start(0, ITEMS)
    users_load.wait()
    own_rows(0, USERS, users_ref[...])
    gather_start(0, USERS)
    pos_load.wait()
    count_load.wait()
    filled = jnp.full((8, HALF), count_ref[0, 0], jnp.int32)
    slot_of = lax.broadcasted_iota(jnp.int32, (8, HALF), 0)
    placed = jnp.full((8, HALF), pos_ref[0, 0], jnp.int32)
    for slot in range(1, SLOTS):
        placed = jnp.where(slot_of == slot, jnp.full((8, HALF), pos_ref[0, slot], jnp.int32), placed)
    meta[core] = jnp.where(slot_of < filled, placed, placed + 64)
    propagate(0)
    dot = functools.partial(jnp.dot, preferred_element_type=F32)
    final_users = 0.5 * (users_ref[...] + scatter_end(0, USERS))
    chosen = dot(user_hot_t[...], split(final_users, 3))
    final_items = 0.5 * (items_ref[...] + scatter_end(0, ITEMS))
    against = dot(item_hot_t[...], split(final_items, 3))
    score = -jnp.sum(chosen * against, axis=1, keepdims=True)
    back = jax.nn.sigmoid(-score)
    hot = user_hot[...]
    grad_users = dot(jnp.concatenate([hot] * 2, axis=1), split(back * against, 2))
    own_rows(1, USERS, grad_users)
    gather_start(1, USERS)
    hot = item_hot[...]
    grad_items = dot(jnp.concatenate([hot] * 2, axis=1), split(back * chosen, 2))
    own_rows(1, ITEMS, grad_items)
    gather_start(1, ITEMS)
    propagate(1)
    out_ref[0] = 0.5 * grad_users + 0.5 * scatter_end(1, USERS)
    out_ref[1] = 0.5 * grad_items + 0.5 * scatter_end(1, ITEMS)
    scatter_sent(1)


def in_hbm(value):
    return pltpu.with_memory_space_constraint(value, pltpu.HBM)


def on_device(users, items, tiles, tile_pos, tile_count, user_ids, pos_ids, neg_ids):
    vmem = pl.BlockSpec(memory_space=pltpu.VMEM)
    dma = pltpu.SemaphoreType.DMA
    batch = user_ids.shape[0]
    cut = (2, ROWS, HALF)
    out = pl.pallas_call(
        kernel,
        out_shape=jax.ShapeDtypeStruct((2, ROWS, WIDTH), F32),
        in_specs=[pl.BlockSpec(memory_space=pl.ANY)] * 8,
        out_specs=vmem,
        scratch_shapes=[
            pltpu.VMEM((ROWS, WIDTH), F32),
            pltpu.VMEM((ROWS, WIDTH), F32),
            pltpu.SMEM((1, SLOTS), jnp.int32),
            pltpu.SMEM((1, 1), jnp.int32),
            pltpu.VMEM((1, batch), jnp.int32),
            pltpu.VMEM((1, batch), jnp.int32),
            pltpu.VMEM((1, batch), jnp.int32),
            pltpu.VMEM((2, SLOTS, TILE, TILE), BF16),
            pltpu.VMEM((2, SLOTS, TILE, TILE), BF16),
            pltpu.VMEM((2, 8, HALF), jnp.int32),
            pltpu.SMEM((2, 8, HALF), jnp.int32),
            pltpu.VMEM((ROWS, batch), BF16),
            pltpu.VMEM((ROWS, batch), BF16),
            pltpu.VMEM((batch, 3 * ROWS), BF16),
            pltpu.VMEM((batch, 3 * ROWS), BF16),
            pltpu.VMEM((4, 4) + cut, BF16),
            pltpu.VMEM((4, 4) + cut, BF16),
            pltpu.VMEM((8, 2) + cut, BF16),
            pltpu.VMEM((8, 2) + cut, BF16),
            pltpu.VMEM((2, 2) + cut, BF16),
            pltpu.VMEM((2 * SLOTS, TILE, HALF), F32),
            pltpu.VMEM((2, BLOCKS) + cut, F32),
            pltpu.VMEM((2, 2, BLOCKS) + cut, BF16),
            pltpu.VMEM((2, 2, 2, 2, 3, ROWS, HALF), BF16),
            pltpu.VMEM((2, 2, 2) + cut, BF16),
            pltpu.VMEM((2, 2, 2) + cut, BF16),
            pltpu.VMEM((2, 2, 2, 2) + cut, BF16),
            pltpu.VMEM((2, 2, 16, ROWS, HALF), BF16),
            dma((8,)),
            dma,
            dma,
            dma,
            dma,
            dma,
            dma((2, 2)),
            dma((2, 2)),
            dma((2, 2, 2)),
            dma((2, 2, 2, 2)),
            dma((2, 2)),
            dma((2, 2)),
            dma((2, 2, 2, 2)),
            dma((2, 2)),
            dma((2, 2)),
            dma((2, 2)),
            dma((2, 2)),
        ],
        compiler_params=pltpu.CompilerParams(
            collective_id=0, has_side_effects=True, vmem_limit_bytes=40 << 20
        ),
        name="propagation_layer",
    )(
        in_hbm(users),
        in_hbm(items),
        in_hbm(tile_pos.reshape(1, SLOTS)),
        tile_count,
        in_hbm(user_ids.reshape(1, batch)),
        in_hbm(pos_ids.reshape(1, batch)),
        in_hbm(neg_ids.reshape(1, batch)),
        in_hbm(tiles.reshape(SLOTS, TILE, TILE)),
    )
    return out[0], out[1]


def solution(mesh):
    placed = (
        P(("row", "col"), None),
        P(("col", "row"), None),
        P("row", "col", None, None, None),
        P("row", "col", None),
        P("row", "col"),
        P(("row", "col")),
        P(("row", "col")),
        P(("row", "col")),
    )
    return jax.shard_map(
        on_device,
        mesh=mesh,
        in_specs=placed,
        out_specs=(P(("row", "col"), None), P(("col", "row"), None)),
        check_vma=False,
    )
```

```python
import functools

import jax
import jax.numpy as jnp
from jax import lax
from jax.experimental import pallas as pl
from jax.experimental.pallas import tpu as pltpu
from jax.sharding import PartitionSpec as P

MESH = pl.DeviceIdType.MESH
BF16 = jnp.bfloat16
F32 = jnp.float32
SLOTS = 4
ROWS = 64
HALF = 128
WIDTH = 256
TILE = 256
RING = 8
BLOCKS = 16
USERS, ITEMS = 0, 1


def split(value, parts):
    terms = []
    for part in range(parts):
        term = value.astype(BF16)
        terms.append(term)
        value = value - term.astype(F32)
    return jnp.concatenate(terms, axis=0)


def kernel(
    users_hbm,
    items_hbm,
    pos_hbm,
    count_hbm,
    uid_hbm,
    pid_hbm,
    nid_hbm,
    tiles_hbm,
    out_ref,
    users_ref,
    items_ref,
    pos_ref,
    count_ref,
    uid_ref,
    pid_ref,
    nid_ref,
    tiles,
    tiles_t,
    meta,
    meta_smem,
    user_hot,
    item_hot,
    user_hot_t,
    item_hot_t,
    user_panel_0,
    user_panel_1,
    item_panel_0,
    item_panel_1,
    stage,
    prod,
    exact,
    sums,
    far,
    relayed,
    last,
    load_sem,
    tile_send,
    tile_recv,
    meta_sem,
    meta_send,
    meta_recv,
    gm_send,
    gm_recv,
    g1_recv,
    g2_recv,
    gb_send,
    gb_recv,
    sf_recv,
    sl_recv,
    s_send,
    sm_send,
):
    row = lax.axis_index("row")
    col = lax.axis_index("col")
    core = lax.rem(row, 2)
    group = row // 2
    mate = (row + 1 - 2 * core, col)
    x_at = (col // RING, group // RING)
    ring_at = (lax.rem(col, RING), lax.rem(group, RING))

    def block(which, other, step):
        x = 1 - x_at[which] if other else x_at[which]
        return x * RING + lax.rem(ring_at[which] + step + RING, RING)

    def device(which, other, step, to_core):
        number = block(which, other, step)
        if which == USERS:
            return (group * 2 + to_core, number)
        return (number * 2 + to_core, col)

    def along(which, step):
        return device(which, False, step, core)

    def send(source, target, send_sem, recv_sem, to):
        pltpu.make_async_remote_copy(
            src_ref=source, dst_ref=target, send_sem=send_sem, recv_sem=recv_sem,
            device_id=to, device_id_type=MESH,
        ).start()

    def awaits(ref, sem):
        pltpu.make_async_remote_copy(
            src_ref=ref, dst_ref=ref, send_sem=sem, recv_sem=sem,
            device_id=mate, device_id_type=MESH,
        ).wait_recv()

    def sent(ref, sem):
        pltpu.make_async_remote_copy(
            src_ref=ref, dst_ref=ref, send_sem=sem, recv_sem=sem,
            device_id=mate, device_id_type=MESH,
        ).wait_send()

    def load(number, source, target):
        copy = pltpu.make_async_copy(source, target, load_sem.at[number])
        copy.start()
        return copy

    items_load = load(0, items_hbm, items_ref)
    users_load = load(1, users_hbm, users_ref)
    pos_load = load(2, pos_hbm, pos_ref)
    count_load = load(3, count_hbm, count_ref)
    ids_load = [
        load(4, uid_hbm, uid_ref), load(5, pid_hbm, pid_ref), load(6, nid_hbm, nid_ref)
    ]
    tiles_load = load(7, tiles_hbm, tiles.at[core])

    barrier = pltpu.get_barrier_semaphore()
    far_steps = [(other, step) for step in (2, -2) for other in (True, False)]
    near_steps = [(False, 1), (False, -1), (True, 0)]
    peers = [mate]
    for which in (USERS, ITEMS):
        for other, step in far_steps + near_steps + [(True, 1), (True, -1)]:
            peers += [device(which, other, step, to_core) for to_core in range(2)]
    for peer in peers:
        pl.semaphore_signal(barrier, 1, device_id=peer, device_id_type=MESH)

    pos_load.wait()
    count_load.wait()
    filled = jnp.full((8, HALF), count_ref[0, 0], jnp.int32)
    slot_of = lax.broadcasted_iota(jnp.int32, (8, HALF), 0)
    placed = jnp.full((8, HALF), pos_ref[0, 0], jnp.int32)
    for slot in range(1, SLOTS):
        placed = jnp.where(slot_of == slot, jnp.full((8, HALF), pos_ref[0, slot], jnp.int32), placed)
    meta[core] = jnp.where(slot_of < filled, placed, placed + 64)

    panels = ((user_panel_0, item_panel_0), (user_panel_1, item_panel_1))

    def at_block(turn, which, number):
        per = 4 if which == USERS else 2
        return panels[turn][which].at[number // per, lax.rem(number, per)]

    def own_rows(turn, which, value):
        stage[turn, which, 0] = value[:, :HALF].astype(BF16)
        stage[turn, which, 1] = value[:, HALF:].astype(BF16)
        own = at_block(turn, which, block(which, False, 0))
        own[core] = stage[turn, which, core]

    def gather_start(turn, which):
        own = at_block(turn, which, block(which, False, 0)).at[core]
        for other, step in far_steps + near_steps:
            if abs(step) == 2:
                sem = g2_recv.at[turn, which, int(other), int(step < 0)]
            elif abs(step) == 1:
                sem = g1_recv.at[turn, which, int(step < 0)]
            else:
                sem = gb_recv.at[turn, which]
            for to_core in range(2):
                send(stage.at[turn, which, to_core], own, gb_send.at[turn, which], sem,
                     device(which, other, step, to_core))
        send(stage.at[turn, which, 1 - core], own,
             gm_send.at[turn, which], gm_recv.at[turn, which], mate)

    def gather_relay(turn, which, other):
        for way, step in ((0, 1), (1, -1)):
            here = at_block(turn, which, block(which, other, -2 * step))
            awaits(here, g2_recv.at[turn, which, int(other), way])
            part = here.at[way]
            send(part, part, gb_send.at[turn, which], gb_recv.at[turn, which], along(which, 2 * step))
            send(here, here, gb_send.at[turn, which], gb_recv.at[turn, which], along(which, step))

    def gather_cross(turn, which):
        for way, step in ((0, 1), (1, -1)):
            here = at_block(turn, which, block(which, False, -step))
            awaits(here, g1_recv.at[turn, which, way])
            send(here, here, gb_send.at[turn, which], gb_recv.at[turn, which],
                 device(which, True, 0, core))

    def gather_end(turn, which):
        awaits(sums.at[turn, which, pl.ds(0, 9)], gb_recv.at[turn, which])
        own = at_block(turn, which, block(which, False, 0))
        awaits(own.at[1 - core], gm_recv.at[turn, which])

    def marks(cell, slot):
        return meta[cell, pl.ds(slot, 1), :]

    def spread_users(turn):
        panel = panels[turn][ITEMS]
        for cell in range(2):
            for slot in range(SLOTS):
                rows = panel[meta_smem[cell, slot, 0] & 7].reshape(TILE, HALF)
                prod[cell * SLOTS + slot] = jnp.dot(
                    tiles[cell, slot], rows, preferred_element_type=F32
                )

        def add(number, carry):
            start = pl.ds(pl.multiple_of(lax.rem(number, 4) * ROWS, ROWS), ROWS)
            for cell in range(2):
                total = jnp.zeros((ROWS, HALF), F32)
                for slot in range(SLOTS):
                    weight = jnp.where((marks(cell, slot) >> 3) == number // 4, 1.0, 0.0)
                    total += weight.astype(F32) * prod[cell * SLOTS + slot, start, :]
                exact[USERS, number, cell] = total
                sums[turn, USERS, number, cell] = total.astype(BF16)
            return carry

        lax.fori_loop(0, BLOCKS, add, 0, unroll=4)

    def spread_items(turn):
        panel = panels[turn][USERS]
        for cell in range(2):
            for slot in range(SLOTS):
                tile = (meta_smem[cell, slot, 0] >> 3) & 3
                rows = panel[tile, :, cell].reshape(TILE, HALF)
                prod[cell * SLOTS + slot] = jnp.dot(
                    tiles_t[cell, slot], rows, preferred_element_type=F32
                )

        def add(number, carry):
            for owner in range(2):
                start = (lax.rem(number, 2) * 2 + owner) * ROWS
                start = pl.ds(pl.multiple_of(start, ROWS), ROWS)
                total = jnp.zeros((ROWS, HALF), F32)
                for cell in range(2):
                    for slot in range(SLOTS):
                        weight = jnp.where((marks(cell, slot) & 71) == number // 2, 1.0, 0.0)
                        total += weight.astype(F32) * prod[cell * SLOTS + slot, start, :]
                exact[ITEMS, number, owner] = total
                sums[turn, ITEMS, number, owner] = total.astype(BF16)
            return carry

        lax.fori_loop(0, BLOCKS, add, 0, unroll=4)

    def scatter_start(turn, which):
        out = s_send.at[turn, which]
        for other in (True, False):
            e = int(other)
            for way, step in ((0, 1), (1, -1)):
                sem = sf_recv.at[turn, which, e, way]
                send(sums.at[turn, which, block(which, other, 4), way],
                     far.at[turn, which, e, way, 2], out, sem, along(which, 2 * step))
                send(sums.at[turn, which, block(which, other, 3 * step)],
                     far.at[turn, which, e, way, pl.ds(0, 2)], out, sem, along(which, step))
        for way, step in ((0, 1), (1, -1)):
            for other in (True, False):
                for to_core in range(2):
                    send_last(turn, which, other, step, 5 * int(other) + 1 + way, to_core,
                              sums.at[turn, which, block(which, other, step), to_core])
        for to_core in range(2):
            send_last(turn, which, True, 0, 5, to_core,
                      sums.at[turn, which, block(which, True, 0), to_core])
        send(sums.at[turn, which, block(which, False, 0), 1 - core],
             last.at[turn, which, core * 10], sm_send.at[turn, which], sl_recv.at[turn, which], mate)

    def send_last(turn, which, other, step, part, to_core, source):
        send(source, last.at[turn, which, core * 10 + part],
             s_send.at[turn, which], sl_recv.at[turn, which], device(which, other, step, to_core))

    def scatter_relay(turn, which, other):
        e = int(other)
        for way, step in ((0, 1), (1, -1)):
            came = far.at[turn, which, e, way]
            awaits(came, sf_recv.at[turn, which, e, way])
            mine = exact.at[which, block(which, other, 2 * step)]
            for owner in range(2):
                total = mine[owner] + came[owner].astype(F32)
                if owner == way:
                    total += came[2].astype(F32)
                relayed[turn, which, e, way, owner] = total.astype(BF16)
            for to_core in range(2):
                send_last(turn, which, other, 2 * step, (8 if other else 3) + way, to_core,
                          relayed.at[turn, which, e, way, to_core])

    def scatter_end(turn, which):
        awaits(last.at[turn, which, pl.ds(0, 19)], sl_recv.at[turn, which])
        last[turn, which, core * 10] = jnp.zeros((ROWS, HALF), BF16)
        own = exact[which, block(which, False, 0), core]
        sides = []
        for side in range(2):
            total = jnp.where(core == side, own, 0.0)
            for part in range(10):
                total += last[turn, which, side * 10 + part].astype(F32)
            sides.append(total)
        return jnp.concatenate(sides, axis=1)

    def prepare():
        user_base = (row * BLOCKS + col) * ROWS
        item_base = (col * 2 * BLOCKS + row) * ROWS
        places = lax.broadcasted_iota(jnp.int32, (ROWS, uid_ref.shape[1]), 0)
        hot = jnp.where(places == uid_ref[...] - user_base, 1.0, 0.0).astype(F32)
        user_hot[...] = hot.astype(BF16)
        user_hot_t[...] = jnp.concatenate([hot] * 3, axis=0).T.astype(BF16)
        hot = jnp.where(places == nid_ref[...] - item_base, 1.0, 0.0).astype(F32)
        hot = hot - jnp.where(places == pid_ref[...] - item_base, 1.0, 0.0).astype(F32)
        item_hot[...] = hot.astype(BF16)
        item_hot_t[...] = jnp.concatenate([hot] * 3, axis=0).T.astype(BF16)

    def gather_sent(turn):
        for which in (USERS, ITEMS):
            sent(stage.at[turn, which, core], gm_send.at[turn, which])
            sent(sums.at[turn, which, pl.ds(0, 15)], gb_send.at[turn, which])

    def scatter_sent(turn):
        for which in (USERS, ITEMS):
            sent(sums.at[turn, which, pl.ds(0, 15)], s_send.at[turn, which])
            sent(stage.at[turn, which, core], sm_send.at[turn, which])

    both = (ITEMS, USERS)

    def propagate(turn):
        if turn == 0:
            send(tiles_hbm, tiles.at[core], tile_send, tile_recv, mate)
            send(meta.at[core], meta.at[core], meta_send, meta_recv, mate)
            for copy in ids_load:
                copy.wait()
            prepare()
        for which in both:
            gather_relay(turn, which, False)
        for which in both:
            gather_cross(turn, which)
        for which in both:
            gather_relay(turn, which, True)
        if turn == 1:
            sent(tiles_hbm, tile_send)
            sent(meta.at[core], meta_send)
            gather_sent(0)
            scatter_sent(0)
        if turn == 0:
            tiles_load.wait()
            awaits(meta.at[1 - core], meta_recv)
            fill = pltpu.make_async_copy(meta, meta_smem, meta_sem)
            fill.start()
            fill.wait()
            awaits(tiles.at[1 - core], tile_recv)
            for cell in range(2):
                for slot in range(SLOTS):
                    tiles_t[cell, slot] = tiles[cell, slot].T
        gather_end(turn, ITEMS)
        spread_users(turn)
        scatter_start(turn, USERS)
        gather_end(turn, USERS)
        spread_items(turn)
        scatter_start(turn, ITEMS)
        for other in (True, False):
            for which in (USERS, ITEMS):
                scatter_relay(turn, which, other)
        if turn == 1:
            gather_sent(1)

    items_load.wait()
    own_rows(0, ITEMS, items_ref[...])
    users_load.wait()
    own_rows(0, USERS, users_ref[...])
    pl.semaphore_wait(barrier, len(peers))
    for which in both:
        gather_start(0, which)
    propagate(0)
    dot = functools.partial(jnp.dot, preferred_element_type=F32)
    final_users = 0.5 * (users_ref[...] + scatter_end(0, USERS))
    chosen = dot(user_hot_t[...], split(final_users, 3))
    final_items = 0.5 * (items_ref[...] + scatter_end(0, ITEMS))
    against = dot(item_hot_t[...], split(final_items, 3))
    score = -jnp.sum(chosen * against, axis=1, keepdims=True)
    back = jax.nn.sigmoid(-score)
    hot = user_hot[...]
    grad_users = dot(jnp.concatenate([hot] * 2, axis=1), split(back * against, 2))
    own_rows(1, USERS, grad_users)
    gather_start(1, USERS)
    hot = item_hot[...]
    grad_items = dot(jnp.concatenate([hot] * 2, axis=1), split(back * chosen, 2))
    own_rows(1, ITEMS, grad_items)
    gather_start(1, ITEMS)
    propagate(1)
    out_ref[0] = 0.5 * grad_users + 0.5 * scatter_end(1, USERS)
    out_ref[1] = 0.5 * grad_items + 0.5 * scatter_end(1, ITEMS)
    scatter_sent(1)


def in_hbm(value):
    return pltpu.with_memory_space_constraint(value, pltpu.HBM)


def on_device(users, items, tiles, tile_pos, tile_count, user_ids, pos_ids, neg_ids):
    vmem = pl.BlockSpec(memory_space=pltpu.VMEM)
    dma = pltpu.SemaphoreType.DMA
    batch = user_ids.shape[0]
    cut = (2, ROWS, HALF)
    out = pl.pallas_call(
        kernel,
        out_shape=jax.ShapeDtypeStruct((2, ROWS, WIDTH), F32),
        in_specs=[pl.BlockSpec(memory_space=pl.ANY)] * 8,
        out_specs=vmem,
        scratch_shapes=[
            pltpu.VMEM((ROWS, WIDTH), F32),
            pltpu.VMEM((ROWS, WIDTH), F32),
            pltpu.SMEM((1, SLOTS), jnp.int32),
            pltpu.SMEM((1, 1), jnp.int32),
            pltpu.VMEM((1, batch), jnp.int32),
            pltpu.VMEM((1, batch), jnp.int32),
            pltpu.VMEM((1, batch), jnp.int32),
            pltpu.VMEM((2, SLOTS, TILE, TILE), BF16),
            pltpu.VMEM((2, SLOTS, TILE, TILE), BF16),
            pltpu.VMEM((2, 8, HALF), jnp.int32),
            pltpu.SMEM((2, 8, HALF), jnp.int32),
            pltpu.VMEM((ROWS, batch), BF16),
            pltpu.VMEM((ROWS, batch), BF16),
            pltpu.VMEM((batch, 3 * ROWS), BF16),
            pltpu.VMEM((batch, 3 * ROWS), BF16),
            pltpu.VMEM((4, 4) + cut, BF16),
            pltpu.VMEM((4, 4) + cut, BF16),
            pltpu.VMEM((8, 2) + cut, BF16),
            pltpu.VMEM((8, 2) + cut, BF16),
            pltpu.VMEM((2, 2) + cut, BF16),
            pltpu.VMEM((2 * SLOTS, TILE, HALF), F32),
            pltpu.VMEM((2, BLOCKS) + cut, F32),
            pltpu.VMEM((2, 2, BLOCKS) + cut, BF16),
            pltpu.VMEM((2, 2, 2, 2, 3, ROWS, HALF), BF16),
            pltpu.VMEM((2, 2, 2, 2) + cut, BF16),
            pltpu.VMEM((2, 2, 20, ROWS, HALF), BF16),
            dma((8,)),
            dma,
            dma,
            dma,
            dma,
            dma,
            dma((2, 2)),
            dma((2, 2)),
            dma((2, 2, 2)),
            dma((2, 2, 2, 2)),
            dma((2, 2)),
            dma((2, 2)),
            dma((2, 2, 2, 2)),
            dma((2, 2)),
            dma((2, 2)),
            dma((2, 2)),
        ],
        compiler_params=pltpu.CompilerParams(
            collective_id=0, has_side_effects=True, vmem_limit_bytes=40 << 20
        ),
        name="propagation_layer",
    )(
        in_hbm(users),
        in_hbm(items),
        in_hbm(tile_pos.reshape(1, SLOTS)),
        tile_count,
        in_hbm(user_ids.reshape(1, batch)),
        in_hbm(pos_ids.reshape(1, batch)),
        in_hbm(neg_ids.reshape(1, batch)),
        in_hbm(tiles.reshape(SLOTS, TILE, TILE)),
    )
    return out[0], out[1]


def solution(mesh):
    placed = (
        P(("row", "col"), None),
        P(("col", "row"), None),
        P("row", "col", None, None, None),
        P("row", "col", None),
        P("row", "col"),
        P(("row", "col")),
        P(("row", "col")),
        P(("row", "col")),
    )
    return jax.shard_map(
        on_device,
        mesh=mesh,
        in_specs=placed,
        out_specs=(P(("row", "col"), None), P(("col", "row"), None)),
        check_vma=False,
    )
```
